256 devices in a mesh: wide: 16 (over z, core), narrow: 16 (over x, y).
Axes of the slice: x: 4, y: 4, z: 8, core: 2. Of those that a mesh axis runs over, the one named last changes fastest.
Arguments:
- traction: float32 [3, 64, 393216], P(None, None, ('wide', 'narrow')), may hold values from -6 to 6
- near_kernel: bfloat16 [768, 4, 512, 512], P(('wide', 'narrow')), may hold values from -0.125 to 0.125
- neighbours: int32 [768, 4], P(('wide', 'narrow')), may hold values from 0 to 767, as said below
- far_basis: bfloat16 [8, 393216, 128], P(None, ('wide', 'narrow')), may hold values from -4 to 4
- surface_gap: float32 [3, 393216], P(None, ('wide', 'narrow')), may hold values from -3 to 3
- friction: float32 [393216], P(('wide', 'narrow')), may hold values from 0.2 to 1
- contact_flags: int32 [393216], P(('wide', 'narrow')), may hold values 0 or 1
- cluster_order: int32 [393216], P(('wide', 'narrow')), may hold values from 0 to 393215, as said below
- approach: float32 [3, 64], replicated, may hold values from -1 to 2
Outputs:
- traction_new: float32 [3, 64, 393216], P(None, None, ('wide', 'narrow'))
- residual: float32 [3, 64, 393216], P(None, None, ('wide', 'narrow'))
- step_size: float32 [64], replicated
The draws below stay inside these ranges and needn't reach their ends.
Inputs may be any that keep to these rules, and one draw needn't show every extreme that they name: `neighbours`: entry 0 of row b is b itself; the other 3 entries are distinct blocks other than b, each within 3 blocks of b. `cluster_order`: a permutation of the panels that maps every aligned group of 1536 panels onto itself.
All inputs are finite; a program needn't handle non-finite values. No bound on the sum of `contact_flags` on one device may be relied on, other than what follows from the above.
Results may differ from the reference program's by a relative error of at most 0.0034.
Values may be sent and summed in bfloat16 or wider, within the bound.
No kernel may reach another device: no remote copies, remote signals or barrier semaphores. Data moves between devices by JAX's collectives and lax.ppermute only.
A program may use at most 64 MiB of HBM per device.

```python
import math
import jax
import jax.numpy as jnp
from jax import lax

C = 64
R = 128
BS = 512
NEAR = 4
BLK_DEV = 3
PAN_DEV = 1536
NBLK = 768
PANELS = 393216
LEVELS = 8


def draw_neighbours(key, part):
    offsets = jnp.concatenate([jnp.arange(-BLK_DEV, 0), jnp.arange(1, BLK_DEV + 1)]).astype(jnp.int32)
    block_ids = jnp.arange(NBLK, dtype=jnp.int32)
    targets = block_ids[:, None] + offsets[None, :]
    valid = (targets >= 0) & (targets < NBLK)
    scores = jax.random.randint(jax.random.fold_in(key, 11), (NBLK, 2 * BLK_DEV), 0, 1 << 16) * (2 * BLK_DEV)
    scores = scores + jnp.arange(2 * BLK_DEV, dtype=jnp.int32)[None, :]
    scores = jnp.where(valid, scores, -1)
    ranked = lax.top_k(scores, NEAR - 1)[1]
    others = jnp.take_along_axis(targets, ranked, axis=1)
    return jnp.concatenate([block_ids[:, None], others], axis=1).astype(jnp.int32)


def draw_cluster_order(key, part):
    groups = PANELS // PAN_DEV
    scores = jax.random.randint(jax.random.fold_in(key, 23), (groups, PAN_DEV), 0, 1 << 16) * PAN_DEV
    scores = scores + jnp.arange(PAN_DEV, dtype=jnp.int32)[None, :]
    shuffled = jnp.argsort(scores, axis=1).astype(jnp.int32)
    offsets = jnp.arange(groups, dtype=jnp.int32)[:, None] * PAN_DEV
    return (shuffled + offsets).reshape(PANELS).astype(jnp.int32)


def place_ends(array, stream_key, low, high):
    extent = array.shape
    place = [jax.random.randint(jax.random.fold_in(stream_key, axis), (), 0, extent[axis]) for axis in range(len(extent))]
    array = array.at[tuple(place)].set(low)
    longest = extent.index(max(extent))
    place[longest] = (place[longest] + 1) % extent[longest]
    return array.at[tuple(place)].set(high)


def levels(own_key, dims, split, smallest, high):
    level, own = 1.0, jax.random.fold_in(own_key, 6)
    for position, parts in split:
        draws = jnp.exp(jax.random.uniform(jax.random.fold_in(own, position), (parts,), jnp.float32, smallest / len(split), high / len(split)))
        level = level * jnp.repeat(draws, dims[position] // parts).reshape([-1 if axis == position else 1 for axis in range(len(dims))])
    return level


def noise(rng, shape, deviation, reach, split=(), kind=jnp.bfloat16):
    factor_of = levels(rng, shape, split, -0.22, 0.18) if split else 1.0
    drawn = jax.random.normal(rng, shape, jnp.float32) * deviation * factor_of
    return jnp.minimum(jnp.maximum(drawn, -reach), reach).astype(kind)


def setup_inputs(seed: int = 0) -> dict:
    splits = jax.random.split(jax.random.key(seed), 10)
    return {
        "traction": noise(splits[0], (3, C, PANELS), 1.0, 6.0, ((2, 256),), jnp.float32),
        "near_kernel": noise(splits[1], (NBLK, NEAR, BS, BS), (NEAR * BS) ** -0.5, 0.125, ((0, 256),)),
        "neighbours": draw_neighbours(jax.random.fold_in(splits[9], 71), 0),
        "far_basis": noise(splits[3], (LEVELS, PANELS, R), 1.0, 4.0, ((1, 256),)),
        "surface_gap": noise(splits[4], (3, PANELS), 0.5, 3.0, ((1, 256),), jnp.float32),
        "friction": jnp.clip(jnp.exp(math.log(1.0) - 1.609438 * jax.random.uniform(splits[5], (PANELS,), jnp.float32) ** levels(splits[5], (PANELS,), ((0, 256),), -0.2, 0.2)), 0.2, 1.0),
        "contact_flags": place_ends((jax.random.randint(splits[6], (PANELS,), 0, 4) < 3).astype(jnp.int32), jax.random.fold_in(splits[6], 1), 0, 1),
        "cluster_order": draw_cluster_order(jax.random.fold_in(splits[9], 71), 0),
        "approach": jnp.clip(jax.random.uniform(splits[8], (3, C), jnp.float32, -1.0, 2.0), -1.0, 2.0),
    }


SLIP_EPS = 0.01

def near_field(field_low, near_kernel, neighbours):
    row_count = field_low.shape[0]
    blocks = field_low.astype(jnp.float32).reshape(row_count, NBLK, BS)

    def one_block(block_id):
        picked = jnp.take(blocks, neighbours[block_id], axis=1)
        weights = near_kernel[block_id].astype(jnp.float32)
        return jnp.einsum('kij,xkj->xi', weights, picked)
    result = lax.map(one_block, jnp.arange(NBLK, dtype=jnp.int32))
    return jnp.transpose(result, (1, 0, 2)).reshape(row_count, PANELS)

def far_field(field_low, far_basis):
    row_count = field_low.shape[0]
    values = field_low.astype(jnp.float32)
    summed = jnp.zeros((row_count, PANELS), jnp.float32)
    for tree_level in range(LEVELS):
        span_len = PAN_DEV * 2 ** (tree_level + 1)
        groups = PANELS // span_len
        factor = far_basis[tree_level].astype(jnp.float32).reshape(groups, span_len, R)
        pieces = values.reshape(row_count, groups, span_len)
        gain = 0.64 / (R * span_len) ** 0.5
        coeffs = (jnp.einsum('xgp,gpr->gxr', pieces, factor) * gain).astype(jnp.bfloat16)
        coeffs = lax.optimization_barrier(coeffs).astype(jnp.float32)
        summed = summed + jnp.einsum('gxr,gpr->xgp', coeffs, factor).reshape(row_count, PANELS)
    return summed

def apply_operator(field, near_kernel, neighbours, far_basis):
    field_low = field.astype(jnp.bfloat16)
    return near_field(field_low, near_kernel, neighbours) + far_field(field_low, far_basis)

def project_cone(trial_point, mu_sorted):
    normal = trial_point[0]
    slide_a = trial_point[1]
    slide_b = trial_point[2]
    slip = jnp.sqrt(slide_a * slide_a + slide_b * slide_b + SLIP_EPS)
    coeff = mu_sorted[None, :]
    stick = slip <= coeff * normal
    pressed = jnp.where(stick, normal, jnp.maximum((normal + coeff * slip) / (1.0 + coeff * coeff), 0.0))
    factor = jnp.where(stick, jnp.ones_like(slip), coeff * pressed / slip)
    return jnp.stack([pressed, factor * slide_a, factor * slide_b])

def reference(traction, near_kernel, neighbours, far_basis, surface_gap, friction, contact_flags, cluster_order, approach):
    gap_sorted = jnp.take(surface_gap, cluster_order, axis=1)
    mu_sorted = jnp.take(friction, cluster_order)
    live_mask = jnp.take(contact_flags, cluster_order).astype(jnp.float32)
    row_count = 3 * C
    state_rows = traction.reshape(row_count, PANELS)
    target = (approach[:, :, None] - gap_sorted[:, None, :]).reshape(row_count, PANELS)
    residual = apply_operator(state_rows, near_kernel, neighbours, far_basis) - target
    image_rows = apply_operator(residual, near_kernel, neighbours, far_basis)
    residual_out = residual.reshape(3, C, PANELS)
    image_out = image_rows.reshape(3, C, PANELS)
    cross_mean = lax.optimization_barrier(jnp.mean(residual_out * image_out, axis=(0, 2)))
    square_mean = lax.optimization_barrier(jnp.mean(image_out * image_out, axis=(0, 2)))
    step_size = cross_mean / (square_mean + 1e-06)
    trial_point = traction - step_size[None, :, None] * residual_out
    updated = project_cone(trial_point, mu_sorted) * live_mask[None, None, :]
    return (updated, residual_out, step_size)
```

```python
import functools
import math

import jax
import jax.numpy as jnp
from jax import lax
from jax.experimental import pallas as pl
from jax.experimental.pallas import tpu as pltpu
from jax.sharding import Mesh
from jax.sharding import PartitionSpec as P

WIDE_NARROW = ("wide_0", "wide_1", "narrow_0", "narrow_1")
NARROW = ("narrow_0", "narrow_1")
WIDE = ("wide_0", "wide_1")

SLIP_EPS = 0.01
COMP = 3
LOADS = 64
ROWS = COMP * LOADS
PAN = 1536
BLK = 512
CHUNKS = PAN // BLK
LEVELS = 8
HALF = LEVELS // 2
RANK = 128
GROUP = 16
QUARTERS = 4
PART = ROWS // QUARTERS

F32 = jnp.float32
BF16 = jnp.bfloat16
NT = (((1,), (1,)), ((), ()))
LIMIT = 48 * 2**20


def gain(level):
    return 0.64 / math.sqrt(RANK * PAN * 2 ** (level + 1))


def call(kernel, name, **kw):
    return pl.pallas_call(
        kernel,
        name=name,
        compiler_params=pltpu.CompilerParams(vmem_limit_bytes=LIMIT),
        **kw,
    )


def whole(shape):
    return pl.BlockSpec(shape, lambda *_: (0,) * len(shape))


SCALARS = pl.BlockSpec(memory_space=pltpu.SMEM)
CHUNK = pl.BlockSpec((ROWS, BLK), lambda b: (0, b))
BASIS = pl.BlockSpec((LEVELS, BLK, RANK), lambda b: (0, b, 0))
PANEL_ROWS = pl.BlockSpec((8, BLK), lambda b: (0, b))
BLOCKWISE = pl.BlockSpec((1, ROWS, BLK), lambda b: (b, 0, 0))


def add_coefs(values, basis_ref, acc_ref, sent_ref):
    step = pl.program_id(0)

    @pl.when(step == 0)
    def _():
        acc_ref[...] = jnp.zeros_like(acc_ref)

    for level in range(HALF):
        pair = jnp.concatenate([basis_ref[level], basis_ref[HALF + level]], axis=1)
        acc_ref[level] += jnp.dot(values, pair, preferred_element_type=F32)

    @pl.when(step == CHUNKS - 1)
    def _():
        for level in range(HALF):
            for quarter in range(QUARTERS):
                rows = pl.ds(quarter * PART, PART)
                slot = level * QUARTERS + quarter
                sent_ref[slot, 0:PART, :] = acc_ref[level, rows, 0:RANK].astype(BF16)
                sent_ref[slot, PART : 2 * PART, :] = acc_ref[level, rows, RANK : 2 * RANK].astype(
                    BF16
                )


def coef_kernel(field_ref, basis_ref, low_ref, sent_ref, acc_ref):
    values = field_ref[...].astype(BF16)
    low_ref[0] = values
    add_coefs(values, basis_ref, acc_ref, sent_ref)


ACC = pltpu.VMEM((HALF, ROWS, 2 * RANK), F32)
SENT = jax.ShapeDtypeStruct((GROUP, 2 * PART, RANK), BF16)
BLOCKS = jax.ShapeDtypeStruct((CHUNKS, ROWS, BLK), BF16)
FIELD = jax.ShapeDtypeStruct((ROWS, PAN), F32)
SUMS = jax.ShapeDtypeStruct((1, 2 * LOADS), F32)


def first_coefs(field, far_basis):
    return call(
        coef_kernel,
        "first_coefs",
        grid=(CHUNKS,),
        in_specs=[CHUNK, BASIS],
        out_specs=[BLOCKWISE, whole(SENT.shape)],
        out_shape=[BLOCKS, SENT],
        scratch_shapes=[ACC],
    )(field, far_basis)


def lower_kernel(place_ref, got_ref, low_ref, up_ref):
    level = place_ref[0] // QUARTERS
    width = 1
    sums = [got_ref[k, 0:PART, :].astype(F32) for k in range(GROUP)]
    while width < GROUP:
        sums = [sums[2 * k] + sums[2 * k + 1] for k in range(len(sums) // 2)]
        width *= 2
        own_level = width.bit_length() - 2

        @pl.when(level == own_level)
        def _(sums=sums, width=width, own_level=own_level):
            for k in range(GROUP):
                low_ref[k] = (sums[k // width] * gain(own_level)).astype(BF16)

    total = got_ref[0, PART : 2 * PART, :].astype(F32)
    for k in range(1, GROUP):
        total += got_ref[k, PART : 2 * PART, :].astype(F32)
    for k in range(GROUP):
        up_ref[k] = total.astype(BF16)


def lower_sums(place, got):
    part = jax.ShapeDtypeStruct((GROUP, PART, RANK), BF16)
    return call(
        lower_kernel,
        "lower_sums",
        in_specs=[SCALARS, whole(SENT.shape)],
        out_specs=[whole(part.shape)] * 2,
        out_shape=[part] * 2,
        grid=(1,),
    )(place, got)


def upper_kernel(place_ref, got_ref, low_ref, sent_ref):
    level = place_ref[0] // QUARTERS
    shift = level + 1
    own = lax.shift_right_logical(place_ref[1], shift)
    total = jnp.zeros((PART, RANK), F32)
    for k in range(GROUP):
        same = (lax.shift_right_logical(jnp.int32(k), shift) == own).astype(F32)
        total += got_ref[k].astype(F32) * same
    scale = jnp.float32(gain(HALF))
    for other in range(1, HALF):
        scale = jnp.where(level == other, jnp.float32(gain(HALF + other)), scale)
    total = (total * scale).astype(BF16)
    for k in range(GROUP):
        sent_ref[k, 0:PART, :] = low_ref[k]
        sent_ref[k, PART : 2 * PART, :] = total


def upper_sums(place, got, low):
    return call(
        upper_kernel,
        "upper_sums",
        in_specs=[SCALARS, whole(got.shape), whole(low.shape)],
        out_specs=whole(SENT.shape),
        out_shape=SENT,
        grid=(1,),
    )(place, got, low)


def near_kernel_body(slots_ref, left_ref, own_ref, right_ref, kernel_ref, *rest):
    out_ref, ext_ref = rest[-2:]
    block = pl.program_id(0)

    @pl.when(block == 0)
    def _():
        ext_ref[0:CHUNKS] = left_ref[...]
        ext_ref[CHUNKS : 2 * CHUNKS] = own_ref[...]
        ext_ref[2 * CHUNKS : 3 * CHUNKS] = right_ref[...]

    total = jnp.zeros((ROWS, BLK), F32)
    for k in range(kernel_ref.shape[1]):
        slot = slots_ref[block, k] - slots_ref[block, 0] + block + CHUNKS
        total += lax.dot_general(ext_ref[slot], kernel_ref[0, k], NT, preferred_element_type=F32)
    if len(rest) == 2:
        out_ref[...] = total
        return
    approach_ref, gap_ref = rest[:2]
    for comp in range(COMP):
        rows = slice(comp * LOADS, (comp + 1) * LOADS)
        out_ref[rows, :] = total[rows] - (approach_ref[rows, :] - gap_ref[comp : comp + 1, :])


def near_field(neighbours, left, own, right, near_kernel, *target):
    specs = [whole((ROWS, 1)), PANEL_ROWS] if target else []
    return call(
        near_kernel_body,
        "near_field",
        grid=(CHUNKS,),
        in_specs=[SCALARS]
        + [whole(BLOCKS.shape)] * 3
        + [pl.BlockSpec((1,) + near_kernel.shape[1:], lambda b: (b, 0, 0, 0))]
        + specs,
        out_specs=CHUNK,
        out_shape=FIELD,
        scratch_shapes=[pltpu.VMEM((3 * CHUNKS, ROWS, BLK), BF16)],
    )(neighbours, left, own, right, near_kernel, *target)


def unpack(got_ref, coef_ref):
    for level in range(HALF):
        for quarter in range(QUARTERS):
            rows = pl.ds(quarter * PART, PART)
            slot = level * QUARTERS + quarter
            coef_ref[rows, level * RANK : (level + 1) * RANK] = got_ref[slot, 0:PART, :]
            coef_ref[rows, (HALF + level) * RANK : (HALF + level + 1) * RANK] = got_ref[
                slot, PART : 2 * PART, :
            ]


def far_field(coef_ref, basis_ref):
    basis = jnp.concatenate([basis_ref[level] for level in range(LEVELS)], axis=1)
    return lax.dot_general(coef_ref[...], basis, NT, preferred_element_type=F32)


COEFS = pltpu.VMEM((ROWS, LEVELS * RANK), BF16)


def residual_kernel(got_ref, near_ref, basis_ref, out_ref, low_ref, sent_ref, coef_ref, acc_ref):
    @pl.when(pl.program_id(0) == 0)
    def _():
        unpack(got_ref, coef_ref)

    residual = far_field(coef_ref, basis_ref) + near_ref[...]
    out_ref[...] = residual
    values = residual.astype(BF16)
    low_ref[0] = values
    add_coefs(values, basis_ref, acc_ref, sent_ref)


def residual_step(got, near, far_basis):
    return call(
        residual_kernel,
        "residual",
        grid=(CHUNKS,),
        in_specs=[whole(SENT.shape), CHUNK, BASIS],
        out_specs=[CHUNK, BLOCKWISE, whole(SENT.shape)],
        out_shape=[FIELD, BLOCKS, SENT],
        scratch_shapes=[COEFS, ACC],
    )(got, near, far_basis)


def product_kernel(got_ref, near_ref, residual_ref, basis_ref, sums_ref, coef_ref, acc_ref):
    step = pl.program_id(0)

    @pl.when(step == 0)
    def _():
        unpack(got_ref, coef_ref)
        acc_ref[...] = jnp.zeros_like(acc_ref)

    image = far_field(coef_ref, basis_ref) + near_ref[...]
    for place, product in enumerate((residual_ref[...] * image, image * image)):
        by_load = product[0:LOADS] + product[LOADS : 2 * LOADS] + product[2 * LOADS : ROWS]
        folded = by_load[:, 0:128]
        for lane in range(128, BLK, 128):
            folded += by_load[:, lane : lane + 128]
        acc_ref[place * LOADS : (place + 1) * LOADS, :] += folded

    @pl.when(step == CHUNKS - 1)
    def _():
        sums_ref[...] = jnp.sum(acc_ref[...].T, axis=0, keepdims=True)


def local_products(got, near, residual, far_basis):
    return call(
        product_kernel,
        "products",
        grid=(CHUNKS,),
        in_specs=[whole(SENT.shape), CHUNK, CHUNK, BASIS],
        out_specs=whole(SUMS.shape),
        out_shape=SUMS,
        scratch_shapes=[COEFS, pltpu.VMEM((2 * LOADS, 128), F32)],
    )(got, near, residual, far_basis)


def sort_kernel(order_ref, values_ref, out_ref):
    rows, cols = values_ref.shape[1], order_ref.shape[1]
    local = lax.rem(order_ref[...], PAN)
    chosen = lax.broadcasted_iota(jnp.int32, (rows, cols), 0) == local
    matrix = jnp.where(chosen, 1.0, 0.0).astype(BF16)
    values = values_ref[...]
    high = values.astype(BF16)
    left_over = values - high.astype(F32)
    middle = left_over.astype(BF16)
    low = (left_over - middle.astype(F32)).astype(BF16)
    out_ref[...] = (
        jnp.dot(high, matrix, preferred_element_type=F32)
        + jnp.dot(middle, matrix, preferred_element_type=F32)
    ) + jnp.dot(low, matrix, preferred_element_type=F32)


def sort_panels(order, values):
    return call(
        sort_kernel,
        "sort_panels",
        grid=(CHUNKS,),
        in_specs=[pl.BlockSpec((1, BLK), lambda b: (0, b)), whole(values.shape)],
        out_specs=PANEL_ROWS,
        out_shape=jax.ShapeDtypeStruct(values.shape, F32),
    )(order, values)


def final_kernel(entries, got_ref, field_ref, residual_ref, sorted_ref, out_ref, step_ref):
    sums = jnp.sum(got_ref[...], axis=0) * (1.0 / entries)
    sums = jnp.broadcast_to(sums, (8, 2 * LOADS))
    square = jnp.concatenate([sums[:, LOADS:], sums[:, LOADS:]], axis=1)
    steps = sums / (square + 1e-06)
    step_ref[...] = steps[0:1]
    column = jnp.concatenate([steps] * 16, axis=0).T[0:LOADS, 0:1]
    normal, slide_a, slide_b = (
        field_ref[rows, :] - column * residual_ref[rows, :]
        for rows in (slice(c * LOADS, (c + 1) * LOADS) for c in range(COMP))
    )
    coeff = sorted_ref[3:4, :]
    live = sorted_ref[4:5, :]
    slip = jnp.sqrt(slide_a * slide_a + slide_b * slide_b + SLIP_EPS)
    stick = slip <= coeff * normal
    slid = jnp.maximum((normal + coeff * slip) / (1.0 + coeff * coeff), 0.0)
    pressed = jnp.where(stick, normal, slid)
    factor = jnp.where(stick, jnp.ones_like(slip), coeff * pressed / slip)
    out_ref[0:LOADS, :] = pressed * live
    out_ref[LOADS : 2 * LOADS, :] = factor * slide_a * live
    out_ref[2 * LOADS : ROWS, :] = factor * slide_b * live


def final_step(got, field, residual, panel_rows, entries):
    return call(
        functools.partial(final_kernel, entries),
        "final",
        grid=(CHUNKS,),
        in_specs=[whole(got.shape), CHUNK, CHUNK, PANEL_ROWS],
        out_specs=[CHUNK, whole(SUMS.shape)],
        out_shape=[FIELD, SUMS],
    )(got, field, residual, panel_rows)


def swap(blocks, axes):
    return lax.all_to_all(blocks, axes, 0, 0)


def beside(blocks):
    size = lax.axis_size(WIDE_NARROW)
    up = [(i, i + 1) for i in range(size - 1)]
    down = [(b, a) for a, b in up]
    return lax.ppermute(blocks, WIDE_NARROW, up), lax.ppermute(blocks, WIDE_NARROW, down)


def tree(place, sent):
    low, up = lower_sums(place, swap(sent, NARROW))
    return swap(upper_sums(place, swap(up, WIDE), low), NARROW)


def body(
    traction,
    near_kernel,
    neighbours,
    far_basis,
    surface_gap,
    friction,
    contact_flags,
    cluster_order,
    approach,
):
    field = traction.reshape(ROWS, PAN)
    place = jnp.stack([lax.axis_index(NARROW), lax.axis_index(WIDE)]).astype(jnp.int32)
    panel_rows = jnp.concatenate(
        [
            surface_gap,
            friction[None],
            contact_flags.astype(F32)[None],
            jnp.zeros((3, PAN), F32),
        ]
    )
    panel_rows = sort_panels(cluster_order[None], panel_rows)

    low, sent = first_coefs(field, far_basis)
    left, right = beside(low)
    near = near_field(
        neighbours, left, low, right, near_kernel, approach.reshape(ROWS, 1), panel_rows
    )
    residual, low, sent = residual_step(tree(place, sent), near, far_basis)
    left, right = beside(low)
    near = near_field(neighbours, left, low, right, near_kernel)
    sums = local_products(tree(place, sent), near, residual, far_basis)

    for axes in (NARROW, WIDE):
        copies = jnp.broadcast_to(sums[None], (GROUP, 1, 2 * LOADS))
        sums = swap(copies, axes)
        if axes is NARROW:
            sums = jnp.sum(sums, axis=0)
    entries = COMP * PAN * lax.axis_size(WIDE_NARROW)
    updated, steps = final_step(sums, field, residual, panel_rows, entries)
    shape = (COMP, LOADS, PAN)
    return updated.reshape(shape), residual.reshape(shape), steps[0, :LOADS]


def solution(mesh):
    finer = Mesh(mesh.devices.reshape(8, 2, 4, 4), ("wide_0", "wide_1", "narrow_0", "narrow_1"))
    placed = (
        P(None, None, WIDE_NARROW),
        P(WIDE_NARROW, None, None, None),
        P(WIDE_NARROW, None),
        P(None, WIDE_NARROW, None),
        P(None, WIDE_NARROW),
        P(WIDE_NARROW),
        P(WIDE_NARROW),
        P(WIDE_NARROW),
        P(),
    )
    return jax.shard_map(
        body,
        mesh=finer,
        in_specs=placed,
        out_specs=(P(None, None, WIDE_NARROW), P(None, None, WIDE_NARROW), P()),
        check_vma=False,
    )
```

```python
import functools
import math

import jax
import jax.numpy as jnp
from jax import lax
from jax.experimental import pallas as pl
from jax.experimental.pallas import tpu as pltpu
from jax.sharding import Mesh
from jax.sharding import PartitionSpec as P

WIDE_NARROW = ("wide_0", "wide_1", "narrow_0", "narrow_1")
NARROW = ("narrow_0", "narrow_1")
WIDE = ("wide_0", "wide_1")

SLIP_EPS = 0.01
COMP = 3
LOADS = 64
ROWS = COMP * LOADS
PAN = 1536
BLK = 512
CHUNKS = PAN // BLK
LEVELS = 8
HALF = LEVELS // 2
RANK = 128
GROUP = 16
QUARTERS = 4
PART = ROWS // QUARTERS

F32 = jnp.float32
BF16 = jnp.bfloat16
NT = (((1,), (1,)), ((), ()))
LIMIT = 16 * 2**20


def gain(level):
    return 0.64 / math.sqrt(RANK * PAN * 2 ** (level + 1))


def call(kernel, name, **kw):
    return pl.pallas_call(
        kernel,
        name=name,
        compiler_params=pltpu.CompilerParams(vmem_limit_bytes=LIMIT),
        **kw,
    )


def whole(shape):
    return pl.BlockSpec(shape, lambda *_: (0,) * len(shape))


SCALARS = pl.BlockSpec(memory_space=pltpu.SMEM)
CHUNK = pl.BlockSpec((ROWS, BLK), lambda b: (0, b))
BASIS = pl.BlockSpec((LEVELS, BLK, RANK), lambda b: (0, b, 0))
PANEL_ROWS = pl.BlockSpec((8, BLK), lambda b: (0, b))
BLOCKWISE = pl.BlockSpec((1, ROWS, BLK), lambda b: (b, 0, 0))


def add_coefs(chunk, values, basis_ref, acc_ref, sent_ref):
    for level in range(HALF):
        pair = jnp.concatenate([basis_ref[level], basis_ref[HALF + level]], axis=1)
        part = jnp.dot(values, pair, preferred_element_type=F32)
        acc_ref[level] = part if chunk == 0 else acc_ref[level] + part
    if chunk < CHUNKS - 1:
        return
    for level in range(HALF):
        for quarter in range(QUARTERS):
            rows = pl.ds(quarter * PART, PART)
            slot = level * QUARTERS + quarter
            sent_ref[slot, 0:PART, :] = acc_ref[level, rows, 0:RANK].astype(BF16)
            sent_ref[slot, PART : 2 * PART, :] = acc_ref[level, rows, RANK : 2 * RANK].astype(BF16)


def coef_kernel(field_hbm, basis_hbm, low_ref, sent_ref, field_ref, basis_ref, acc_ref, sems):
    copies = []
    for chunk in range(CHUNKS):
        panels = pl.ds(chunk * BLK, BLK)
        copies.append(
            (
                pltpu.make_async_copy(
                    field_hbm.at[:, panels], field_ref.at[chunk], sems.at[0, chunk]
                ),
                pltpu.make_async_copy(
                    basis_hbm.at[:, panels, :], basis_ref.at[chunk], sems.at[1, chunk]
                ),
            )
        )
        for copy in copies[-1]:
            copy.start()
    for chunk in range(CHUNKS):
        for copy in copies[chunk]:
            copy.wait()
        values = field_ref[chunk].astype(BF16)
        low_ref[chunk] = values
        add_coefs(chunk, values, basis_ref.at[chunk], acc_ref, sent_ref)


ACC = pltpu.VMEM((HALF, ROWS, 2 * RANK), F32)
SENT = jax.ShapeDtypeStruct((GROUP, 2 * PART, RANK), BF16)
BLOCKS = jax.ShapeDtypeStruct((CHUNKS, ROWS, BLK), BF16)
FIELD = jax.ShapeDtypeStruct((ROWS, PAN), F32)
SUMS = jax.ShapeDtypeStruct((1, 2 * LOADS), F32)


def first_coefs(field, far_basis):
    return call(
        coef_kernel,
        "first_coefs",
        in_specs=[pl.BlockSpec(memory_space=pltpu.HBM)] * 2,
        out_specs=[pl.BlockSpec(memory_space=pltpu.VMEM)] * 2,
        out_shape=[BLOCKS, SENT],
        scratch_shapes=[
            pltpu.VMEM((CHUNKS, ROWS, BLK), F32),
            pltpu.VMEM((CHUNKS, LEVELS, BLK, RANK), BF16),
            ACC,
            pltpu.SemaphoreType.DMA((2, CHUNKS)),
        ],
    )(field, far_basis)


def lower_kernel(place_ref, got_ref, low_ref, up_ref):
    level = place_ref[0] // QUARTERS
    width = 1
    sums = [got_ref[k, 0:PART, :].astype(F32) for k in range(GROUP)]
    while width < GROUP:
        sums = [sums[2 * k] + sums[2 * k + 1] for k in range(len(sums) // 2)]
        width *= 2
        own_level = width.bit_length() - 2

        @pl.when(level == own_level)
        def _(sums=sums, width=width, own_level=own_level):
            for k in range(GROUP):
                low_ref[k] = (sums[k // width] * gain(own_level)).astype(BF16)

    total = got_ref[0, PART : 2 * PART, :].astype(F32)
    for k in range(1, GROUP):
        total += got_ref[k, PART : 2 * PART, :].astype(F32)
    for k in range(GROUP):
        up_ref[k] = total.astype(BF16)


def lower_sums(place, got):
    part = jax.ShapeDtypeStruct((GROUP, PART, RANK), BF16)
    return call(
        lower_kernel,
        "lower_sums",
        in_specs=[SCALARS, whole(SENT.shape)],
        out_specs=[whole(part.shape)] * 2,
        out_shape=[part] * 2,
        grid=(1,),
    )(place, got)


def upper_kernel(place_ref, got_ref, low_ref, sent_ref):
    level = place_ref[0] // QUARTERS
    shift = level + 1
    own = lax.shift_right_logical(place_ref[1], shift)
    total = jnp.zeros((PART, RANK), F32)
    for k in range(GROUP):
        same = (lax.shift_right_logical(jnp.int32(k), shift) == own).astype(F32)
        total += got_ref[k].astype(F32) * same
    scale = jnp.float32(gain(HALF))
    for other in range(1, HALF):
        scale = jnp.where(level == other, jnp.float32(gain(HALF + other)), scale)
    total = (total * scale).astype(BF16)
    for k in range(GROUP):
        sent_ref[k, 0:PART, :] = low_ref[k]
        sent_ref[k, PART : 2 * PART, :] = total


def upper_sums(place, got, low):
    return call(
        upper_kernel,
        "upper_sums",
        in_specs=[SCALARS, whole(got.shape), whole(low.shape)],
        out_specs=whole(SENT.shape),
        out_shape=SENT,
        grid=(1,),
    )(place, got, low)


def near_kernel_body(slots_ref, left_ref, own_ref, right_ref, kernel_ref, *rest):
    out_ref, ext_ref = rest[-2:]
    block = pl.program_id(0)

    @pl.when(block == 0)
    def _():
        ext_ref[0:CHUNKS] = left_ref[...]
        ext_ref[CHUNKS : 2 * CHUNKS] = own_ref[...]
        ext_ref[2 * CHUNKS : 3 * CHUNKS] = right_ref[...]

    total = jnp.zeros((ROWS, BLK), F32)
    for k in range(kernel_ref.shape[1]):
        slot = slots_ref[block, k] - slots_ref[block, 0] + block + CHUNKS
        total += lax.dot_general(ext_ref[slot], kernel_ref[0, k], NT, preferred_element_type=F32)
    if len(rest) == 2:
        out_ref[...] = total
        return
    approach_ref, gap_ref = rest[:2]
    for comp in range(COMP):
        rows = slice(comp * LOADS, (comp + 1) * LOADS)
        out_ref[rows, :] = total[rows] - (approach_ref[rows, :] - gap_ref[comp : comp + 1, :])


def near_field(neighbours, left, own, right, near_kernel, *target):
    specs = [whole((ROWS, 1)), PANEL_ROWS] if target else []
    return call(
        near_kernel_body,
        "near_field",
        grid=(CHUNKS,),
        in_specs=[SCALARS]
        + [whole(BLOCKS.shape)] * 3
        + [pl.BlockSpec((1,) + near_kernel.shape[1:], lambda b: (b, 0, 0, 0))]
        + specs,
        out_specs=CHUNK,
        out_shape=FIELD,
        scratch_shapes=[pltpu.VMEM((3 * CHUNKS, ROWS, BLK), BF16)],
    )(neighbours, left, own, right, near_kernel, *target)


def unpack(got_ref, coef_ref):
    for level in range(HALF):
        for quarter in range(QUARTERS):
            rows = pl.ds(quarter * PART, PART)
            slot = level * QUARTERS + quarter
            coef_ref[rows, level * RANK : (level + 1) * RANK] = got_ref[slot, 0:PART, :]
            coef_ref[rows, (HALF + level) * RANK : (HALF + level + 1) * RANK] = got_ref[
                slot, PART : 2 * PART, :
            ]


def far_field(coef_ref, basis_ref):
    basis = jnp.concatenate([basis_ref[level] for level in range(LEVELS)], axis=1)
    return lax.dot_general(coef_ref[...], basis, NT, preferred_element_type=F32)


COEFS = pltpu.VMEM((ROWS, LEVELS * RANK), BF16)


def residual_kernel(got_ref, near_ref, basis_ref, out_ref, low_ref, sent_ref, coef_ref, acc_ref):
    unpack(got_ref, coef_ref)
    for chunk in range(CHUNKS):
        panels = pl.ds(chunk * BLK, BLK)
        part = basis_ref.at[:, panels, :]
        residual = far_field(coef_ref, part) + near_ref[:, panels]
        out_ref[:, panels] = residual
        values = residual.astype(BF16)
        low_ref[chunk] = values
        add_coefs(chunk, values, part, acc_ref, sent_ref)


IN_VMEM = pl.BlockSpec(memory_space=pltpu.VMEM)


def residual_step(got, near, far_basis):
    return call(
        residual_kernel,
        "residual",
        in_specs=[IN_VMEM] * 3,
        out_specs=[IN_VMEM] * 3,
        out_shape=[FIELD, BLOCKS, SENT],
        scratch_shapes=[COEFS, ACC],
    )(got, near, far_basis)


def product_kernel(got_ref, near_ref, residual_ref, basis_ref, sums_ref, coef_ref, acc_ref):
    step = pl.program_id(0)

    @pl.when(step == 0)
    def _():
        unpack(got_ref, coef_ref)
        acc_ref[...] = jnp.zeros_like(acc_ref)

    image = far_field(coef_ref, basis_ref) + near_ref[...]
    for place, product in enumerate((residual_ref[...] * image, image * image)):
        by_load = product[0:LOADS] + product[LOADS : 2 * LOADS] + product[2 * LOADS : ROWS]
        folded = by_load[:, 0:128]
        for lane in range(128, BLK, 128):
            folded += by_load[:, lane : lane + 128]
        acc_ref[place * LOADS : (place + 1) * LOADS, :] += folded

    @pl.when(step == CHUNKS - 1)
    def _():
        sums_ref[...] = jnp.sum(acc_ref[...].T, axis=0, keepdims=True)


def local_products(got, near, residual, far_basis):
    return call(
        product_kernel,
        "products",
        grid=(CHUNKS,),
        in_specs=[whole(SENT.shape), CHUNK, CHUNK, BASIS],
        out_specs=whole(SUMS.shape),
        out_shape=SUMS,
        scratch_shapes=[COEFS, pltpu.VMEM((2 * LOADS, 128), F32)],
    )(got, near, residual, far_basis)


def sort_kernel(order_ref, values_ref, out_ref):
    rows, cols = values_ref.shape[1], order_ref.shape[1]
    local = lax.rem(order_ref[...], PAN)
    chosen = lax.broadcasted_iota(jnp.int32, (rows, cols), 0) == local
    matrix = jnp.where(chosen, 1.0, 0.0).astype(BF16)
    values = values_ref[...]
    high = values.astype(BF16)
    left_over = values - high.astype(F32)
    middle = left_over.astype(BF16)
    low = (left_over - middle.astype(F32)).astype(BF16)
    out_ref[...] = (
        jnp.dot(high, matrix, preferred_element_type=F32)
        + jnp.dot(middle, matrix, preferred_element_type=F32)
    ) + jnp.dot(low, matrix, preferred_element_type=F32)


def sort_panels(order, values):
    return call(
        sort_kernel,
        "sort_panels",
        grid=(CHUNKS,),
        in_specs=[pl.BlockSpec((1, BLK), lambda b: (0, b)), whole(values.shape)],
        out_specs=PANEL_ROWS,
        out_shape=jax.ShapeDtypeStruct(values.shape, F32),
    )(order, values)


def final_kernel(entries, got_ref, field_ref, residual_ref, sorted_ref, out_ref, step_ref):
    sums = jnp.sum(got_ref[...], axis=0) * (1.0 / entries)
    sums = jnp.broadcast_to(sums, (8, 2 * LOADS))
    square = jnp.concatenate([sums[:, LOADS:], sums[:, LOADS:]], axis=1)
    steps = sums / (square + 1e-06)
    step_ref[...] = steps[0:1]
    column = jnp.concatenate([steps] * 16, axis=0).T[0:LOADS, 0:1]
    normal, slide_a, slide_b = (
        field_ref[rows, :] - column * residual_ref[rows, :]
        for rows in (slice(c * LOADS, (c + 1) * LOADS) for c in range(COMP))
    )
    coeff = sorted_ref[3:4, :]
    live = sorted_ref[4:5, :]
    slip = jnp.sqrt(slide_a * slide_a + slide_b * slide_b + SLIP_EPS)
    stick = slip <= coeff * normal
    slid = jnp.maximum((normal + coeff * slip) / (1.0 + coeff * coeff), 0.0)
    pressed = jnp.where(stick, normal, slid)
    factor = jnp.where(stick, jnp.ones_like(slip), coeff * pressed / slip)
    out_ref[0:LOADS, :] = pressed * live
    out_ref[LOADS : 2 * LOADS, :] = factor * slide_a * live
    out_ref[2 * LOADS : ROWS, :] = factor * slide_b * live


def final_step(got, field, residual, panel_rows, entries):
    return call(
        functools.partial(final_kernel, entries),
        "final",
        grid=(CHUNKS,),
        in_specs=[whole(got.shape), CHUNK, CHUNK, PANEL_ROWS],
        out_specs=[CHUNK, whole(SUMS.shape)],
        out_shape=[FIELD, SUMS],
    )(got, field, residual, panel_rows)


def swap(blocks, axes):
    return lax.all_to_all(blocks, axes, 0, 0)


def beside(blocks):
    size = lax.axis_size(WIDE_NARROW)
    up = [(i, i + 1) for i in range(size - 1)]
    down = [(b, a) for a, b in up]
    return lax.ppermute(blocks, WIDE_NARROW, up), lax.ppermute(blocks, WIDE_NARROW, down)


def tree(place, sent):
    low, up = lower_sums(place, swap(sent, NARROW))
    return swap(upper_sums(place, swap(up, WIDE), low), NARROW)


def body(
    traction,
    near_kernel,
    neighbours,
    far_basis,
    surface_gap,
    friction,
    contact_flags,
    cluster_order,
    approach,
):
    field = traction.reshape(ROWS, PAN)
    place = jnp.stack([lax.axis_index(NARROW), lax.axis_index(WIDE)]).astype(jnp.int32)
    panel_rows = jnp.concatenate(
        [
            surface_gap,
            friction[None],
            contact_flags.astype(F32)[None],
            jnp.zeros((3, PAN), F32),
        ]
    )
    panel_rows = sort_panels(cluster_order[None], panel_rows)

    low, sent = first_coefs(field, far_basis)
    left, right = beside(low)
    near = near_field(
        neighbours, left, low, right, near_kernel, approach.reshape(ROWS, 1), panel_rows
    )
    residual, low, sent = residual_step(tree(place, sent), near, far_basis)
    left, right = beside(low)
    near = near_field(neighbours, left, low, right, near_kernel)
    sums = local_products(tree(place, sent), near, residual, far_basis)

    devices = lax.axis_size(WIDE_NARROW)
    sums = swap(jnp.broadcast_to(sums[None], (devices, 1, 2 * LOADS)), WIDE_NARROW)
    entries = COMP * PAN * devices
    updated, steps = final_step(sums, field, residual, panel_rows, entries)
    shape = (COMP, LOADS, PAN)
    return updated.reshape(shape), residual.reshape(shape), steps[0, :LOADS]


def solution(mesh):
    finer = Mesh(mesh.devices.reshape(8, 2, 4, 4), ("wide_0", "wide_1", "narrow_0", "narrow_1"))
    placed = (
        P(None, None, WIDE_NARROW),
        P(WIDE_NARROW, None, None, None),
        P(WIDE_NARROW, None),
        P(None, WIDE_NARROW, None),
        P(None, WIDE_NARROW),
        P(WIDE_NARROW),
        P(WIDE_NARROW),
        P(WIDE_NARROW),
        P(),
    )
    return jax.shard_map(
        body,
        mesh=finer,
        in_specs=placed,
        out_specs=(P(None, None, WIDE_NARROW), P(None, None, WIDE_NARROW), P()),
        check_vma=False,
    )
```

```python
import functools
import math

import jax
import jax.numpy as jnp
from jax import lax
from jax.experimental import pallas as pl
from jax.experimental.pallas import tpu as pltpu
from jax.sharding import Mesh
from jax.sharding import PartitionSpec as P

WIDE_NARROW = ("wide_0", "wide_1", "narrow_0", "narrow_1")
NARROW = ("narrow_0", "narrow_1")
WIDE = ("wide_0", "wide_1")

SLIP_EPS = 0.01
COMP = 3
LOADS = 64
ROWS = COMP * LOADS
PAN = 1536
BLK = 512
CHUNKS = PAN // BLK
LEVELS = 8
HALF = LEVELS // 2
RANK = 128
GROUP = 16
QUARTERS = 4
PART = ROWS // QUARTERS

F32 = jnp.float32
BF16 = jnp.bfloat16
NT = (((1,), (1,)), ((), ()))
LIMIT = 16 * 2**20


def gain(level):
    return 0.64 / math.sqrt(RANK * PAN * 2 ** (level + 1))


def call(kernel, name, **kw):
    return pl.pallas_call(
        kernel,
        name=name,
        compiler_params=pltpu.CompilerParams(vmem_limit_bytes=LIMIT),
        **kw,
    )


def in_vmem(array):
    return pltpu.with_memory_space_constraint(array, pltpu.VMEM)


def in_hbm(array):
    return pltpu.with_memory_space_constraint(array, pltpu.HBM)


def whole(shape):
    return pl.BlockSpec(shape, lambda *_: (0,) * len(shape))


SCALARS = pl.BlockSpec(memory_space=pltpu.SMEM)
IN_VMEM = pl.BlockSpec(memory_space=pltpu.VMEM)
IN_HBM = pl.BlockSpec(memory_space=pltpu.HBM)
CHUNK = pl.BlockSpec((ROWS, BLK), lambda b: (0, b))
BASIS = pl.BlockSpec((LEVELS, BLK, RANK), lambda b: (0, b, 0))
PANEL_ROWS = pl.BlockSpec((8, BLK), lambda b: (0, b))
BLOCKWISE = pl.BlockSpec((1, ROWS, BLK), lambda b: (b, 0, 0))


def add_coefs(chunk, values, basis_ref, acc_ref, sent_ref):
    for level in range(HALF):
        pair = jnp.concatenate([basis_ref[level], basis_ref[HALF + level]], axis=1)
        part = jnp.dot(values, pair, preferred_element_type=F32)
        acc_ref[level] = part if chunk == 0 else acc_ref[level] + part
    if chunk < CHUNKS - 1:
        return
    for level in range(HALF):
        for quarter in range(QUARTERS):
            rows = pl.ds(quarter * PART, PART)
            slot = level * QUARTERS + quarter
            sent_ref[slot, 0:PART, :] = acc_ref[level, rows, 0:RANK].astype(BF16)
            sent_ref[slot, PART : 2 * PART, :] = acc_ref[level, rows, RANK : 2 * RANK].astype(BF16)


def coef_kernel(field_hbm, basis_hbm, low_ref, sent_ref, field_ref, basis_ref, acc_ref, sems):
    copies = []
    for chunk in range(CHUNKS):
        panels = pl.ds(chunk * BLK, BLK)
        copies.append(
            (
                pltpu.make_async_copy(
                    field_hbm.at[:, panels], field_ref.at[chunk], sems.at[0, chunk]
                ),
                pltpu.make_async_copy(
                    basis_hbm.at[:, panels, :], basis_ref.at[chunk], sems.at[1, chunk]
                ),
            )
        )
        for copy in copies[-1]:
            copy.start()
    for chunk in range(CHUNKS):
        for copy in copies[chunk]:
            copy.wait()
        values = field_ref[chunk].astype(BF16)
        low_ref[chunk] = values
        add_coefs(chunk, values, basis_ref.at[chunk], acc_ref, sent_ref)


ACC = pltpu.VMEM((HALF, ROWS, 2 * RANK), F32)
SENT = pltpu.HBM((GROUP, 2 * PART, RANK), BF16)
BLOCKS = pltpu.HBM((CHUNKS, ROWS, BLK), BF16)
FIELD = pltpu.HBM((ROWS, PAN), F32)
SUMS = jax.ShapeDtypeStruct((1, 2 * LOADS), F32)


def first_coefs(field, far_basis):
    return call(
        coef_kernel,
        "first_coefs",
        in_specs=[IN_HBM] * 2,
        out_specs=[IN_VMEM] * 2,
        out_shape=[BLOCKS, SENT],
        scratch_shapes=[
            pltpu.VMEM((CHUNKS, ROWS, BLK), F32),
            pltpu.VMEM((CHUNKS, LEVELS, BLK, RANK), BF16),
            ACC,
            pltpu.SemaphoreType.DMA((2, CHUNKS)),
        ],
    )(in_hbm(field), in_hbm(far_basis))


def lower_kernel(place_ref, got_ref, low_ref, up_ref):
    level = place_ref[0] // QUARTERS
    width = 1
    sums = [got_ref[k, 0:PART, :].astype(F32) for k in range(GROUP)]
    while width < GROUP:
        sums = [sums[2 * k] + sums[2 * k + 1] for k in range(len(sums) // 2)]
        width *= 2
        own_level = width.bit_length() - 2

        @pl.when(level == own_level)
        def _(sums=sums, width=width, own_level=own_level):
            for k in range(GROUP):
                low_ref[k] = (sums[k // width] * gain(own_level)).astype(BF16)

    total = got_ref[0, PART : 2 * PART, :].astype(F32)
    for k in range(1, GROUP):
        total += got_ref[k, PART : 2 * PART, :].astype(F32)
    for k in range(GROUP):
        up_ref[k] = total.astype(BF16)


def lower_sums(place, got):
    part = pltpu.HBM((GROUP, PART, RANK), BF16)
    return call(
        lower_kernel,
        "lower_sums",
        in_specs=[SCALARS, whole(SENT.shape)],
        out_specs=[whole(part.shape)] * 2,
        out_shape=[part] * 2,
        grid=(1,),
    )(place, got)


def upper_kernel(place_ref, got_ref, low_ref, sent_ref):
    level = place_ref[0] // QUARTERS
    shift = level + 1
    own = lax.shift_right_logical(place_ref[1], shift)
    total = jnp.zeros((PART, RANK), F32)
    for k in range(GROUP):
        same = (lax.shift_right_logical(jnp.int32(k), shift) == own).astype(F32)
        total += got_ref[k].astype(F32) * same
    scale = jnp.float32(gain(HALF))
    for other in range(1, HALF):
        scale = jnp.where(level == other, jnp.float32(gain(HALF + other)), scale)
    total = (total * scale).astype(BF16)
    for k in range(GROUP):
        sent_ref[k, 0:PART, :] = low_ref[k]
        sent_ref[k, PART : 2 * PART, :] = total


def upper_sums(place, got, low):
    return call(
        upper_kernel,
        "upper_sums",
        in_specs=[SCALARS, whole(got.shape), whole(low.shape)],
        out_specs=whole(SENT.shape),
        out_shape=SENT,
        grid=(1,),
    )(place, got, low)


def near_kernel_body(slots_ref, left_hbm, own_hbm, right_hbm, kernel_hbm, *rest):
    out_ref, ext_ref, kernel_ref, ext_sems, kernel_sems = rest[-5:]
    block = pl.program_id(0)

    def sides():
        for side, source in enumerate((own_hbm, left_hbm, right_hbm)):
            place = ((1, 0, 2)[side]) * CHUNKS
            yield pltpu.make_async_copy(
                source, ext_ref.at[pl.ds(place, CHUNKS)], ext_sems.at[side]
            )

    def kernel_copy(at):
        return pltpu.make_async_copy(kernel_hbm.at[at], kernel_ref.at[at], kernel_sems.at[at])

    @pl.when(block == 0)
    def _():
        for copy in sides():
            copy.start()
        for at in range(CHUNKS):
            kernel_copy(at).start()
        for copy in sides():
            copy.wait()

    kernel_copy(block).wait()
    total = jnp.zeros((ROWS, BLK), F32)
    for k in range(kernel_ref.shape[1]):
        slot = slots_ref[block, k] - slots_ref[block, 0] + block + CHUNKS
        total += lax.dot_general(
            ext_ref[slot], kernel_ref[block, k], NT, preferred_element_type=F32
        )
    if len(rest) == 5:
        out_ref[...] = total
        return
    approach_ref, gap_ref = rest[:2]
    square = (LOADS, LOADS)
    diagonal = lax.broadcasted_iota(jnp.int32, square, 0) == lax.broadcasted_iota(
        jnp.int32, square, 1
    )
    for comp in range(COMP):
        rows = slice(comp * LOADS, (comp + 1) * LOADS)
        row = jnp.broadcast_to(approach_ref[comp : comp + 1, :], square)
        column = jnp.sum(jnp.where(diagonal, row, 0.0), axis=1, keepdims=True)
        out_ref[rows, :] = total[rows] - (column - gap_ref[comp : comp + 1, :])


def near_field(neighbours, left, own, right, near_kernel, *target):
    specs = [whole((COMP, LOADS)), PANEL_ROWS] if target else []
    return call(
        near_kernel_body,
        "near_field",
        grid=(CHUNKS,),
        in_specs=[SCALARS] + [IN_HBM] * 4 + specs,
        out_specs=CHUNK,
        out_shape=FIELD,
        scratch_shapes=[
            pltpu.VMEM((3 * CHUNKS, ROWS, BLK), BF16),
            pltpu.VMEM(near_kernel.shape, BF16),
            pltpu.SemaphoreType.DMA((3,)),
            pltpu.SemaphoreType.DMA((CHUNKS,)),
        ],
    )(neighbours, *map(in_hbm, (left, own, right, near_kernel)), *target)


def unpack(got_ref, coef_ref):
    for level in range(HALF):
        for quarter in range(QUARTERS):
            rows = pl.ds(quarter * PART, PART)
            slot = level * QUARTERS + quarter
            coef_ref[rows, level * RANK : (level + 1) * RANK] = got_ref[slot, 0:PART, :]
            coef_ref[rows, (HALF + level) * RANK : (HALF + level + 1) * RANK] = got_ref[
                slot, PART : 2 * PART, :
            ]


def far_field(coef_ref, basis_ref):
    basis = jnp.concatenate([basis_ref[level] for level in range(LEVELS)], axis=1)
    return lax.dot_general(coef_ref[...], basis, NT, preferred_element_type=F32)


COEFS = pltpu.VMEM((ROWS, LEVELS * RANK), BF16)


def residual_kernel(
    got_ref, near_hbm, basis_ref, out_hbm, low_hbm, sent_ref, *scratch
):
    near_ref, out_ref, low_ref, coef_ref, acc_ref, sems = scratch

    arriving, leaving = [], []
    for chunk in range(CHUNKS):
        panels = pl.ds(chunk * BLK, BLK)
        copy = pltpu.make_async_copy(
            near_hbm.at[:, panels], near_ref.at[chunk], sems.at[0, chunk]
        )
        copy.start()
        arriving.append(copy)
    unpack(got_ref, coef_ref)
    for chunk in range(CHUNKS):
        panels = pl.ds(chunk * BLK, BLK)
        part = basis_ref.at[:, panels, :]
        far = far_field(coef_ref, part)
        arriving[chunk].wait()
        residual = far + near_ref[chunk]
        out_ref[chunk] = residual
        values = residual.astype(BF16)
        low_ref[chunk] = values
        for copy in (
            pltpu.make_async_copy(out_ref.at[chunk], out_hbm.at[:, panels], sems.at[1, chunk]),
            pltpu.make_async_copy(low_ref.at[chunk], low_hbm.at[chunk], sems.at[2, chunk]),
        ):
            copy.start()
            leaving.append(copy)
        add_coefs(chunk, values, part, acc_ref, sent_ref)
    for copy in leaving:
        copy.wait()


def residual_step(got, near, far_basis):
    return call(
        residual_kernel,
        "residual",
        in_specs=[IN_VMEM, IN_HBM, IN_VMEM],
        out_specs=[IN_HBM, IN_HBM, IN_VMEM],
        out_shape=[FIELD, BLOCKS, SENT],
        scratch_shapes=[
            pltpu.VMEM((CHUNKS, ROWS, BLK), F32),
            pltpu.VMEM((CHUNKS, ROWS, BLK), F32),
            pltpu.VMEM((CHUNKS, ROWS, BLK), BF16),
            COEFS,
            ACC,
            pltpu.SemaphoreType.DMA((3, CHUNKS)),
        ],
    )(in_vmem(got), in_hbm(near), in_vmem(far_basis))


def product_kernel(got_ref, near_ref, residual_ref, basis_ref, sums_ref, coef_ref, acc_ref):
    step = pl.program_id(0)

    @pl.when(step == 0)
    def _():
        unpack(got_ref, coef_ref)
        acc_ref[...] = jnp.zeros_like(acc_ref)

    image = far_field(coef_ref, basis_ref) + near_ref[...]
    for place, product in enumerate((residual_ref[...] * image, image * image)):
        by_load = product[0:LOADS] + product[LOADS : 2 * LOADS] + product[2 * LOADS : ROWS]
        folded = by_load[:, 0:128]
        for lane in range(128, BLK, 128):
            folded += by_load[:, lane : lane + 128]
        acc_ref[place * LOADS : (place + 1) * LOADS, :] += folded

    @pl.when(step == CHUNKS - 1)
    def _():
        sums_ref[...] = jnp.sum(acc_ref[...].T, axis=0, keepdims=True)


def local_products(got, near, residual, far_basis):
    return call(
        product_kernel,
        "products",
        grid=(CHUNKS,),
        in_specs=[whole(SENT.shape), CHUNK, CHUNK, BASIS],
        out_specs=whole(SUMS.shape),
        out_shape=SUMS,
        scratch_shapes=[COEFS, pltpu.VMEM((2 * LOADS, 128), F32)],
    )(in_vmem(got), in_hbm(near), in_hbm(residual), in_vmem(far_basis))


def sort_kernel(order_ref, values_ref, out_ref):
    rows, cols = values_ref.shape[1], order_ref.shape[1]
    local = lax.rem(order_ref[...], PAN)
    chosen = lax.broadcasted_iota(jnp.int32, (rows, cols), 0) == local
    matrix = jnp.where(chosen, 1.0, 0.0).astype(BF16)
    values = values_ref[...]
    high = values.astype(BF16)
    left_over = values - high.astype(F32)
    middle = left_over.astype(BF16)
    low = (left_over - middle.astype(F32)).astype(BF16)
    out_ref[...] = (
        jnp.dot(high, matrix, preferred_element_type=F32)
        + jnp.dot(middle, matrix, preferred_element_type=F32)
    ) + jnp.dot(low, matrix, preferred_element_type=F32)


def sort_panels(order, values):
    return call(
        sort_kernel,
        "sort_panels",
        grid=(CHUNKS,),
        in_specs=[pl.BlockSpec((1, BLK), lambda b: (0, b)), whole(values.shape)],
        out_specs=PANEL_ROWS,
        out_shape=jax.ShapeDtypeStruct(values.shape, F32),
    )(order, values)


def final_kernel(entries, got_ref, field_ref, residual_ref, sorted_ref, out_ref, step_ref):
    sums = jnp.sum(got_ref[...], axis=0) * (1.0 / entries)
    sums = jnp.broadcast_to(sums, (8, 2 * LOADS))
    square = jnp.concatenate([sums[:, LOADS:], sums[:, LOADS:]], axis=1)
    steps = sums / (square + 1e-06)
    step_ref[...] = steps[0, 0:LOADS]
    column = jnp.concatenate([steps] * 16, axis=0).T[0:LOADS, 0:1]
    normal, slide_a, slide_b = (
        field_ref[rows, :] - column * residual_ref[rows, :]
        for rows in (slice(c * LOADS, (c + 1) * LOADS) for c in range(COMP))
    )
    coeff = sorted_ref[3:4, :]
    live = sorted_ref[4:5, :]
    slip = jnp.sqrt(slide_a * slide_a + slide_b * slide_b + SLIP_EPS)
    stick = slip <= coeff * normal
    slid = jnp.maximum((normal + coeff * slip) / (1.0 + coeff * coeff), 0.0)
    pressed = jnp.where(stick, normal, slid)
    factor = jnp.where(stick, jnp.ones_like(slip), coeff * pressed / slip)
    out_ref[0:LOADS, :] = pressed * live
    out_ref[LOADS : 2 * LOADS, :] = factor * slide_a * live
    out_ref[2 * LOADS : ROWS, :] = factor * slide_b * live


def final_step(got, field, residual, panel_rows, entries):
    return call(
        functools.partial(final_kernel, entries),
        "final",
        grid=(CHUNKS,),
        in_specs=[whole(got.shape), CHUNK, CHUNK, PANEL_ROWS],
        out_specs=[CHUNK, whole((LOADS,))],
        out_shape=[FIELD, jax.ShapeDtypeStruct((LOADS,), F32)],
    )(got, in_hbm(field), in_hbm(residual), panel_rows)


def swap(blocks, axes):
    return lax.all_to_all(blocks, axes, 0, 0)


def beside(blocks):
    size = lax.axis_size(WIDE_NARROW)
    up = [(i, i + 1) for i in range(size - 1)]
    down = [(b, a) for a, b in up]
    return lax.ppermute(blocks, WIDE_NARROW, up), lax.ppermute(blocks, WIDE_NARROW, down)


def operator(place, low, sent, near_field_of):
    left, right = beside(low)
    lower, up = lower_sums(place, swap(sent, NARROW))
    near = near_field_of(left, low, right)
    upper, near = lax.optimization_barrier((swap(up, WIDE), near))
    return near, swap(upper_sums(place, upper, lower), NARROW)


def body(
    traction,
    near_kernel,
    neighbours,
    far_basis,
    surface_gap,
    friction,
    contact_flags,
    cluster_order,
    approach,
):
    field = traction.reshape(ROWS, PAN)
    place = jnp.stack([lax.axis_index(NARROW), lax.axis_index(WIDE)]).astype(jnp.int32)
    panel_rows = jnp.concatenate(
        [
            surface_gap,
            friction[None],
            contact_flags.astype(F32)[None],
            jnp.zeros((3, PAN), F32),
        ]
    )
    panel_rows = sort_panels(cluster_order[None], panel_rows)

    def near_of(*target):
        return lambda left, own, right: near_field(
            neighbours, left, own, right, near_kernel, *target
        )

    low, sent = first_coefs(field, far_basis)
    near, coefs = operator(place, low, sent, near_of(approach, panel_rows))
    residual, low, sent = residual_step(coefs, near, far_basis)
    near, coefs = operator(place, low, sent, near_of())
    sums = local_products(coefs, near, residual, far_basis)

    devices = lax.axis_size(WIDE_NARROW)
    sums = swap(jnp.broadcast_to(sums[None], (devices, 1, 2 * LOADS)), WIDE_NARROW)
    entries = COMP * PAN * devices
    updated, steps = final_step(sums, field, residual, panel_rows, entries)
    shape = (COMP, LOADS, PAN)
    return updated.reshape(shape), residual.reshape(shape), steps


def solution(mesh):
    finer = Mesh(mesh.devices.reshape(8, 2, 4, 4), ("wide_0", "wide_1", "narrow_0", "narrow_1"))
    placed = (
        P(None, None, WIDE_NARROW),
        P(WIDE_NARROW, None, None, None),
        P(WIDE_NARROW, None),
        P(None, WIDE_NARROW, None),
        P(None, WIDE_NARROW),
        P(WIDE_NARROW),
        P(WIDE_NARROW),
        P(WIDE_NARROW),
        P(),
    )
    return jax.shard_map(
        body,
        mesh=finer,
        in_specs=placed,
        out_specs=(P(None, None, WIDE_NARROW), P(None, None, WIDE_NARROW), P()),
        check_vma=False,
    )
```

```python
import functools
import math

import jax
import jax.numpy as jnp
from jax import lax
from jax.experimental import pallas as pl
from jax.experimental.pallas import tpu as pltpu
from jax.sharding import Mesh
from jax.sharding import PartitionSpec as P

WIDE_NARROW = ("wide_0", "wide_1", "narrow_0", "narrow_1")
NARROW = ("narrow_0", "narrow_1")
WIDE = ("wide_0", "wide_1")

SLIP_EPS = 0.01
COMP = 3
LOADS = 64
ROWS = COMP * LOADS
PAN = 1536
BLK = 512
CHUNKS = PAN // BLK
LEVELS = 8
HALF = LEVELS // 2
RANK = 128
GROUP = 16
QUARTERS = 4
PART = ROWS // QUARTERS

F32 = jnp.float32
BF16 = jnp.bfloat16
NT = (((1,), (1,)), ((), ()))
LIMIT = 16 * 2**20


def gain(level):
    return 0.64 / math.sqrt(RANK * PAN * 2 ** (level + 1))


def call(kernel, name, **kw):
    return pl.pallas_call(
        kernel,
        name=name,
        compiler_params=pltpu.CompilerParams(vmem_limit_bytes=LIMIT),
        **kw,
    )


def in_vmem(array):
    return pltpu.with_memory_space_constraint(array, pltpu.VMEM)


def in_hbm(array):
    return pltpu.with_memory_space_constraint(array, pltpu.HBM)


def whole(shape):
    return pl.BlockSpec(shape, lambda *_: (0,) * len(shape))


SCALARS = pl.BlockSpec(memory_space=pltpu.SMEM)
IN_VMEM = pl.BlockSpec(memory_space=pltpu.VMEM)
IN_HBM = pl.BlockSpec(memory_space=pltpu.HBM)
CHUNK = pl.BlockSpec((ROWS, BLK), lambda b: (0, b))
PANEL_ROWS = pl.BlockSpec((8, BLK), lambda b: (0, b))


def send_coefs(level, values, pair, sent_ref, sent_hbm, sem):
    coefs = jnp.dot(values, pair, preferred_element_type=F32).astype(BF16)
    for quarter in range(QUARTERS):
        rows = slice(quarter * PART, (quarter + 1) * PART)
        slot = level * QUARTERS + quarter
        sent_ref[slot, 0:PART, :] = coefs[rows, 0:RANK]
        sent_ref[slot, PART : 2 * PART, :] = coefs[rows, RANK : 2 * RANK]
    slots = pl.ds(level * QUARTERS, QUARTERS)
    copy = pltpu.make_async_copy(sent_ref.at[slots], sent_hbm.at[slots], sem)
    copy.start()
    return copy


def coef_kernel(field_hbm, basis_hbm, low_hbm, sent_hbm, *scratch):
    field_ref, low_ref, basis_ref, sent_ref, field_sems, basis_sems, low_sems, sent_sems = scratch
    fields, bases, leaving = [], [], []
    for chunk in range(CHUNKS):
        panels = pl.ds(chunk * BLK, BLK)
        fields.append(
            pltpu.make_async_copy(
                field_hbm.at[:, panels], field_ref.at[chunk], field_sems.at[chunk]
            )
        )
        fields[-1].start()
    for level in range(HALF):
        bases.append(
            [
                pltpu.make_async_copy(basis_hbm.at[at], basis_ref.at[at], basis_sems.at[at])
                for at in (level, HALF + level)
            ]
        )
        for copy in bases[-1]:
            copy.start()
    for chunk in range(CHUNKS):
        fields[chunk].wait()
        low_ref[chunk] = field_ref[chunk].astype(BF16)
        copy = pltpu.make_async_copy(low_ref.at[chunk], low_hbm.at[chunk], low_sems.at[chunk])
        copy.start()
        leaving.append(copy)
    values = jnp.concatenate([low_ref[chunk] for chunk in range(CHUNKS)], axis=1)
    for level in range(HALF):
        for copy in bases[level]:
            copy.wait()
        pair = jnp.concatenate([basis_ref[level], basis_ref[HALF + level]], axis=1)
        leaving.append(send_coefs(level, values, pair, sent_ref, sent_hbm, sent_sems.at[level]))
    for copy in leaving:
        copy.wait()


SENT = pltpu.HBM((GROUP, 2 * PART, RANK), BF16)
BLOCKS = pltpu.HBM((CHUNKS, ROWS, BLK), BF16)
FIELD = pltpu.HBM((ROWS, PAN), F32)
SUMS = jax.ShapeDtypeStruct((1, 2 * LOADS), F32)


def first_coefs(field, far_basis):
    return call(
        coef_kernel,
        "first_coefs",
        in_specs=[IN_HBM] * 2,
        out_specs=[IN_HBM] * 2,
        out_shape=[BLOCKS, SENT],
        scratch_shapes=[
            pltpu.VMEM((CHUNKS, ROWS, BLK), F32),
            pltpu.VMEM(BLOCKS.shape, BF16),
            pltpu.VMEM((LEVELS, PAN, RANK), BF16),
            pltpu.VMEM(SENT.shape, BF16),
            pltpu.SemaphoreType.DMA((CHUNKS,)),
            pltpu.SemaphoreType.DMA((LEVELS,)),
            pltpu.SemaphoreType.DMA((CHUNKS,)),
            pltpu.SemaphoreType.DMA((HALF,)),
        ],
    )(in_hbm(field), in_hbm(far_basis))


LOWER, UPPER = pl.ds(0, PART), pl.ds(PART, PART)


def lower_kernel(place_ref, got_ref, back_hbm, up_hbm, low_ref, up_ref, sems):
    total = got_ref[0, UPPER, :].astype(F32)
    for k in range(1, GROUP):
        total += got_ref[k, UPPER, :].astype(F32)
    total = total.astype(BF16)
    for k in range(GROUP):
        up_ref[k] = total
    up_copy = pltpu.make_async_copy(up_ref, up_hbm, sems.at[0])
    up_copy.start()
    level = place_ref[0] // QUARTERS
    width = 1
    sums = [got_ref[k, LOWER, :].astype(F32) for k in range(GROUP)]
    while width < GROUP:
        sums = [sums[2 * k] + sums[2 * k + 1] for k in range(len(sums) // 2)]
        width *= 2
        own_level = width.bit_length() - 2

        @pl.when(level == own_level)
        def _(sums=sums, width=width, own_level=own_level):
            for k in range(GROUP):
                low_ref[k] = (sums[k // width] * gain(own_level)).astype(BF16)

    low_copy = pltpu.make_async_copy(low_ref, back_hbm.at[:, LOWER, :], sems.at[1])
    low_copy.start()
    up_copy.wait()
    low_copy.wait()


def lower_sums(place, got):
    part = (GROUP, PART, RANK)
    return call(
        lower_kernel,
        "lower_sums",
        in_specs=[SCALARS, IN_VMEM],
        out_specs=[IN_HBM] * 2,
        out_shape=[SENT, pltpu.HBM(part, BF16)],
        scratch_shapes=[
            pltpu.VMEM(part, BF16),
            pltpu.VMEM(part, BF16),
            pltpu.SemaphoreType.DMA((2,)),
        ],
    )(place, in_vmem(got))


def upper_kernel(place_ref, got_ref, _, back_hbm, up_ref, sem):
    level = place_ref[0] // QUARTERS
    shift = level + 1
    own = lax.shift_right_logical(place_ref[1], shift)
    total = jnp.zeros((PART, RANK), F32)
    for k in range(GROUP):
        same = (lax.shift_right_logical(jnp.int32(k), shift) == own).astype(F32)
        total += got_ref[k].astype(F32) * same
    scale = jnp.float32(gain(HALF))
    for other in range(1, HALF):
        scale = jnp.where(level == other, jnp.float32(gain(HALF + other)), scale)
    total = (total * scale).astype(BF16)
    for k in range(GROUP):
        up_ref[k] = total
    copy = pltpu.make_async_copy(up_ref, back_hbm.at[:, UPPER, :], sem.at[0])
    copy.start()
    copy.wait()


def upper_sums(place, got, back):
    return call(
        upper_kernel,
        "upper_sums",
        in_specs=[SCALARS, IN_VMEM, IN_HBM],
        out_specs=IN_HBM,
        out_shape=SENT,
        input_output_aliases={2: 0},
        scratch_shapes=[
            pltpu.VMEM((GROUP, PART, RANK), BF16),
            pltpu.SemaphoreType.DMA((1,)),
        ],
    )(place, in_vmem(got), in_hbm(back))


def near_kernel_body(slots_ref, left_hbm, own_hbm, right_hbm, kernel_hbm, *rest):
    out_ref, ext_ref, kernel_ref, ext_sems, kernel_sems = rest[-5:]
    block = pl.program_id(0)

    def sides():
        for side, source in enumerate((own_hbm, left_hbm, right_hbm)):
            place = ((1, 0, 2)[side]) * CHUNKS
            yield pltpu.make_async_copy(
                source, ext_ref.at[pl.ds(place, CHUNKS)], ext_sems.at[side]
            )

    def kernel_copy(at):
        return pltpu.make_async_copy(kernel_hbm.at[at], kernel_ref.at[at], kernel_sems.at[at])

    @pl.when(block == 0)
    def _():
        for copy in sides():
            copy.start()
        for at in range(CHUNKS):
            kernel_copy(at).start()
        for copy in sides():
            copy.wait()

    kernel_copy(block).wait()
    total = jnp.zeros((ROWS, BLK), F32)
    for k in range(kernel_ref.shape[1]):
        slot = slots_ref[block, k] - slots_ref[block, 0] + block + CHUNKS
        total += lax.dot_general(
            ext_ref[slot], kernel_ref[block, k], NT, preferred_element_type=F32
        )
    if len(rest) == 5:
        out_ref[...] = total
        return
    approach_ref, gap_ref = rest[:2]
    square = (LOADS, LOADS)
    diagonal = lax.broadcasted_iota(jnp.int32, square, 0) == lax.broadcasted_iota(
        jnp.int32, square, 1
    )
    for comp in range(COMP):
        rows = slice(comp * LOADS, (comp + 1) * LOADS)
        row = jnp.broadcast_to(approach_ref[comp : comp + 1, :], square)
        column = jnp.sum(jnp.where(diagonal, row, 0.0), axis=1, keepdims=True)
        out_ref[rows, :] = total[rows] - (column - gap_ref[comp : comp + 1, :])


def near_field(neighbours, left, own, right, near_kernel, *target):
    specs = [whole((COMP, LOADS)), PANEL_ROWS] if target else []
    return call(
        near_kernel_body,
        "near_field",
        grid=(CHUNKS,),
        in_specs=[SCALARS] + [IN_HBM] * 4 + specs,
        out_specs=CHUNK,
        out_shape=FIELD,
        scratch_shapes=[
            pltpu.VMEM((3 * CHUNKS, ROWS, BLK), BF16),
            pltpu.VMEM(near_kernel.shape, BF16),
            pltpu.SemaphoreType.DMA((3,)),
            pltpu.SemaphoreType.DMA((CHUNKS,)),
        ],
    )(neighbours, *map(in_hbm, (left, own, right, near_kernel)), *target)


def unpack(got_ref, coef_ref):
    for level in range(HALF):
        for quarter in range(QUARTERS):
            rows = pl.ds(quarter * PART, PART)
            slot = level * QUARTERS + quarter
            coef_ref[rows, level * RANK : (level + 1) * RANK] = got_ref[slot, 0:PART, :]
            coef_ref[rows, (HALF + level) * RANK : (HALF + level + 1) * RANK] = got_ref[
                slot, PART : 2 * PART, :
            ]


def far_field(coef_ref, basis_ref):
    basis = jnp.concatenate([basis_ref[level] for level in range(LEVELS)], axis=1)
    return lax.dot_general(coef_ref[...], basis, NT, preferred_element_type=F32)


COEFS = pltpu.VMEM((ROWS, LEVELS * RANK), BF16)


def start_chunks(source_hbm, ref, sems, row):
    copies = []
    for chunk in range(CHUNKS):
        copy = pltpu.make_async_copy(
            source_hbm.at[:, pl.ds(chunk * BLK, BLK)], ref.at[chunk], sems.at[row, chunk]
        )
        copy.start()
        copies.append(copy)
    return copies


def residual_kernel(got_ref, near_hbm, basis_ref, out_hbm, low_hbm, sent_hbm, *scratch):
    near_ref, out_ref, low_ref, sent_ref, coef_ref, sems, sent_sems = scratch
    arriving = start_chunks(near_hbm, near_ref, sems, 0)
    leaving = []
    unpack(got_ref, coef_ref)
    for chunk in range(CHUNKS):
        panels = pl.ds(chunk * BLK, BLK)
        far = far_field(coef_ref, basis_ref.at[:, panels, :])
        arriving[chunk].wait()
        residual = far + near_ref[chunk]
        out_ref[chunk] = residual
        low_ref[chunk] = residual.astype(BF16)
        for copy in (
            pltpu.make_async_copy(out_ref.at[chunk], out_hbm.at[:, panels], sems.at[1, chunk]),
            pltpu.make_async_copy(low_ref.at[chunk], low_hbm.at[chunk], sems.at[2, chunk]),
        ):
            copy.start()
            leaving.append(copy)
    values = jnp.concatenate([low_ref[chunk] for chunk in range(CHUNKS)], axis=1)
    for level in range(HALF):
        pair = jnp.concatenate([basis_ref[level], basis_ref[HALF + level]], axis=1)
        leaving.append(send_coefs(level, values, pair, sent_ref, sent_hbm, sent_sems.at[level]))
    for copy in leaving:
        copy.wait()


def residual_step(got, near, far_basis):
    return call(
        residual_kernel,
        "residual",
        in_specs=[IN_VMEM, IN_HBM, IN_VMEM],
        out_specs=[IN_HBM] * 3,
        out_shape=[FIELD, BLOCKS, SENT],
        scratch_shapes=[
            pltpu.VMEM((CHUNKS, ROWS, BLK), F32),
            pltpu.VMEM((CHUNKS, ROWS, BLK), F32),
            pltpu.VMEM(BLOCKS.shape, BF16),
            pltpu.VMEM(SENT.shape, BF16),
            COEFS,
            pltpu.SemaphoreType.DMA((3, CHUNKS)),
            pltpu.SemaphoreType.DMA((HALF,)),
        ],
    )(in_vmem(got), in_hbm(near), in_vmem(far_basis))


def product_kernel(got_ref, near_hbm, residual_hbm, basis_ref, sums_ref, *scratch):
    near_ref, residual_ref, coef_ref, sems = scratch
    nears = start_chunks(near_hbm, near_ref, sems, 0)
    residuals = start_chunks(residual_hbm, residual_ref, sems, 1)
    unpack(got_ref, coef_ref)
    totals = [jnp.zeros((LOADS, 128), F32)] * 2
    for chunk in range(CHUNKS):
        far = far_field(coef_ref, basis_ref.at[:, pl.ds(chunk * BLK, BLK), :])
        nears[chunk].wait()
        residuals[chunk].wait()
        image = far + near_ref[chunk]
        for place, product in enumerate((residual_ref[chunk] * image, image * image)):
            by_load = product[0:LOADS] + product[LOADS : 2 * LOADS] + product[2 * LOADS : ROWS]
            for lane in range(0, BLK, 128):
                totals[place] += by_load[:, lane : lane + 128]
    sums_ref[...] = jnp.sum(jnp.concatenate(totals, axis=0).T, axis=0, keepdims=True)


def local_products(got, near, residual, far_basis):
    return call(
        product_kernel,
        "products",
        in_specs=[IN_VMEM, IN_HBM, IN_HBM, IN_VMEM],
        out_specs=IN_VMEM,
        out_shape=SUMS,
        scratch_shapes=[
            pltpu.VMEM((CHUNKS, ROWS, BLK), F32),
            pltpu.VMEM((CHUNKS, ROWS, BLK), F32),
            COEFS,
            pltpu.SemaphoreType.DMA((2, CHUNKS)),
        ],
    )(in_vmem(got), in_hbm(near), in_hbm(residual), in_vmem(far_basis))


def sort_kernel(order_ref, values_ref, out_ref):
    rows, cols = values_ref.shape[1], order_ref.shape[1]
    local = lax.rem(order_ref[...], PAN)
    chosen = lax.broadcasted_iota(jnp.int32, (rows, cols), 0) == local
    matrix = jnp.where(chosen, 1.0, 0.0).astype(BF16)
    values = values_ref[...]
    high = values.astype(BF16)
    left_over = values - high.astype(F32)
    middle = left_over.astype(BF16)
    low = (left_over - middle.astype(F32)).astype(BF16)
    out_ref[...] = (
        jnp.dot(high, matrix, preferred_element_type=F32)
        + jnp.dot(middle, matrix, preferred_element_type=F32)
    ) + jnp.dot(low, matrix, preferred_element_type=F32)


def sort_panels(order, values):
    return call(
        sort_kernel,
        "sort_panels",
        grid=(CHUNKS,),
        in_specs=[pl.BlockSpec((1, BLK), lambda b: (0, b)), whole(values.shape)],
        out_specs=PANEL_ROWS,
        out_shape=pltpu.HBM(values.shape, F32),
    )(order, values)


def final_kernel(entries, got_ref, field_ref, residual_ref, sorted_ref, out_hbm, *rest):
    step_ref, out_ref, sems = rest
    sums = jnp.sum(got_ref[...], axis=0) * (1.0 / entries)
    sums = jnp.broadcast_to(sums, (8, 2 * LOADS))
    square = jnp.concatenate([sums[:, LOADS:], sums[:, LOADS:]], axis=1)
    steps = sums / (square + 1e-06)
    step_ref[...] = steps[0, 0:LOADS]
    column = jnp.concatenate([steps] * 16, axis=0).T[0:LOADS, 0:1]
    comps = [slice(c * LOADS, (c + 1) * LOADS) for c in range(COMP)]
    leaving = []
    for chunk in range(CHUNKS):
        panels = pl.ds(chunk * BLK, BLK)
        normal, slide_a, slide_b = (
            field_ref[rows, panels] - column * residual_ref[rows, panels] for rows in comps
        )
        coeff = sorted_ref[3:4, panels]
        live = sorted_ref[4:5, panels]
        slip = jnp.sqrt(slide_a * slide_a + slide_b * slide_b + SLIP_EPS)
        stick = slip <= coeff * normal
        slid = jnp.maximum((normal + coeff * slip) / (1.0 + coeff * coeff), 0.0)
        pressed = jnp.where(stick, normal, slid)
        factor = jnp.where(stick, jnp.ones_like(slip), coeff * pressed / slip)
        out_ref[chunk, comps[0], :] = pressed * live
        out_ref[chunk, comps[1], :] = factor * slide_a * live
        out_ref[chunk, comps[2], :] = factor * slide_b * live
        copy = pltpu.make_async_copy(out_ref.at[chunk], out_hbm.at[:, panels], sems.at[chunk])
        copy.start()
        leaving.append(copy)
    for copy in leaving:
        copy.wait()


def final_step(got, field, residual, panel_rows, entries):
    return call(
        functools.partial(final_kernel, entries),
        "final",
        in_specs=[IN_VMEM] * 4,
        out_specs=[IN_HBM, IN_VMEM],
        out_shape=[FIELD, jax.ShapeDtypeStruct((LOADS,), F32)],
        scratch_shapes=[
            pltpu.VMEM((CHUNKS, ROWS, BLK), F32),
            pltpu.SemaphoreType.DMA((CHUNKS,)),
        ],
    )(in_vmem(got), in_vmem(field), in_vmem(residual), in_vmem(panel_rows))


def swap(blocks, axes):
    return lax.all_to_all(blocks, axes, 0, 0)


def beside(blocks):
    size = lax.axis_size(WIDE_NARROW)
    up = [(i, i + 1) for i in range(size - 1)]
    down = [(b, a) for a, b in up]
    return lax.ppermute(blocks, WIDE_NARROW, up), lax.ppermute(blocks, WIDE_NARROW, down)


def operator(place, low, sent, *early):
    sides = beside(low)
    lower, up = lower_sums(place, swap(sent, NARROW))
    upper, sides, early = lax.optimization_barrier((swap(up, WIDE), sides, early))
    return sides, swap(upper_sums(place, upper, lower), NARROW), early


def body(
    traction,
    near_kernel,
    neighbours,
    far_basis,
    surface_gap,
    friction,
    contact_flags,
    cluster_order,
    approach,
):
    field = traction.reshape(ROWS, PAN)
    place = jnp.stack([lax.axis_index(NARROW), lax.axis_index(WIDE)]).astype(jnp.int32)
    panel_rows = jnp.concatenate(
        [
            surface_gap,
            friction[None],
            contact_flags.astype(F32)[None],
            jnp.zeros((3, PAN), F32),
        ]
    )
    panel_rows = sort_panels(cluster_order[None], panel_rows)

    low, sent = first_coefs(field, far_basis)
    (left, right), coefs, (panel_rows,) = operator(place, low, sent, panel_rows)
    near = near_field(
        neighbours, left, low, right, near_kernel, approach, in_hbm(panel_rows)
    )
    residual, low, sent = residual_step(coefs, near, far_basis)
    (left, right), coefs, _ = operator(place, low, sent)
    near = near_field(neighbours, left, low, right, near_kernel)
    sums = local_products(coefs, near, residual, far_basis)

    devices = lax.axis_size(WIDE_NARROW)
    sums = swap(jnp.broadcast_to(sums[None], (devices, 1, 2 * LOADS)), WIDE_NARROW)
    entries = COMP * PAN * devices
    updated, steps = final_step(sums, field, residual, panel_rows, entries)
    shape = (COMP, LOADS, PAN)
    return updated.reshape(shape), residual.reshape(shape), steps


def solution(mesh):
    finer = Mesh(mesh.devices.reshape(8, 2, 4, 4), ("wide_0", "wide_1", "narrow_0", "narrow_1"))
    placed = (
        P(None, None, WIDE_NARROW),
        P(WIDE_NARROW, None, None, None),
        P(WIDE_NARROW, None),
        P(None, WIDE_NARROW, None),
        P(None, WIDE_NARROW),
        P(WIDE_NARROW),
        P(WIDE_NARROW),
        P(WIDE_NARROW),
        P(),
    )
    return jax.shard_map(
        body,
        mesh=finer,
        in_specs=placed,
        out_specs=(P(None, None, WIDE_NARROW), P(None, None, WIDE_NARROW), P()),
        check_vma=False,
    )
```

```python
import functools
import math

import jax
import jax.numpy as jnp
from jax import lax
from jax.experimental import pallas as pl
from jax.experimental.pallas import tpu as pltpu
from jax.sharding import Mesh
from jax.sharding import PartitionSpec as P

WIDE_NARROW = ("wide_0", "wide_1", "narrow_0", "narrow_1")
NARROW = ("narrow_0", "narrow_1")
WIDE = ("wide_0", "wide_1")

SLIP_EPS = 0.01
COMP = 3
LOADS = 64
ROWS = COMP * LOADS
PAN = 1536
BLK = 512
CHUNKS = PAN // BLK
LEVELS = 8
HALF = LEVELS // 2
RANK = 128
GROUP = 16
QUARTERS = 4
PART = ROWS // QUARTERS

F32 = jnp.float32
BF16 = jnp.bfloat16
NT = (((1,), (1,)), ((), ()))
LIMIT = 16 * 2**20
IN_FLIGHT = 5


def gain(level):
    return 0.64 / math.sqrt(RANK * PAN * 2 ** (level + 1))


def call(kernel, name, **kw):
    return pl.pallas_call(
        kernel,
        name=name,
        compiler_params=pltpu.CompilerParams(vmem_limit_bytes=LIMIT),
        **kw,
    )


def in_vmem(array):
    return pltpu.with_memory_space_constraint(array, pltpu.VMEM)


def in_hbm(array):
    return pltpu.with_memory_space_constraint(array, pltpu.HBM)


def whole(shape):
    return pl.BlockSpec(shape, lambda *_: (0,) * len(shape))


SCALARS = pl.BlockSpec(memory_space=pltpu.SMEM)
IN_VMEM = pl.BlockSpec(memory_space=pltpu.VMEM)
IN_HBM = pl.BlockSpec(memory_space=pltpu.HBM)
CHUNK = pl.BlockSpec((ROWS, BLK), lambda b: (0, b))
PANEL_ROWS = pl.BlockSpec((8, BLK), lambda b: (0, b))


def send_coefs(level, coefs, sent_ref, sent_hbm, sem):
    coefs = coefs.astype(BF16)
    for quarter in range(QUARTERS):
        rows = slice(quarter * PART, (quarter + 1) * PART)
        slot = level * QUARTERS + quarter
        sent_ref[slot, 0:PART, :] = coefs[rows, 0:RANK]
        sent_ref[slot, PART : 2 * PART, :] = coefs[rows, RANK : 2 * RANK]
    slots = pl.ds(level * QUARTERS, QUARTERS)
    copy = pltpu.make_async_copy(sent_ref.at[slots], sent_hbm.at[slots], sem)
    copy.start()
    return copy


def coef_kernel(field_hbm, basis_hbm, low_hbm, sent_hbm, *scratch):
    field_ref, low_ref, basis_ref, acc_ref, sent_ref, sems, sent_sems = scratch
    arriving, leaving = [], []
    for chunk in range(CHUNKS):
        panels = pl.ds(chunk * BLK, BLK)
        arriving.append(
            (
                pltpu.make_async_copy(
                    field_hbm.at[:, panels], field_ref.at[chunk], sems.at[0, chunk]
                ),
                pltpu.make_async_copy(
                    basis_hbm.at[:, panels, :], basis_ref.at[chunk], sems.at[1, chunk]
                ),
            )
        )
        for copy in arriving[-1]:
            copy.start()
    for chunk in range(CHUNKS):
        for copy in arriving[chunk]:
            copy.wait()
        values = field_ref[chunk].astype(BF16)
        low_ref[chunk] = values
        copy = pltpu.make_async_copy(low_ref.at[chunk], low_hbm.at[chunk], sems.at[2, chunk])
        copy.start()
        leaving.append(copy)
        for level in range(HALF):
            pair = jnp.concatenate(
                [basis_ref[chunk, level], basis_ref[chunk, HALF + level]], axis=1
            )
            part = jnp.dot(values, pair, preferred_element_type=F32)
            if chunk > 0:
                part += acc_ref[level]
            if chunk < CHUNKS - 1:
                acc_ref[level] = part
            else:
                leaving.append(send_coefs(level, part, sent_ref, sent_hbm, sent_sems.at[level]))
    for copy in leaving:
        copy.wait()


SENT = pltpu.HBM((GROUP, 2 * PART, RANK), BF16)
BLOCKS = pltpu.HBM((CHUNKS, ROWS, BLK), BF16)
FIELD = pltpu.HBM((ROWS, PAN), F32)
SUMS = jax.ShapeDtypeStruct((1, 2 * LOADS), F32)


def first_coefs(field, far_basis):
    return call(
        coef_kernel,
        "first_coefs",
        in_specs=[IN_HBM] * 2,
        out_specs=[IN_HBM] * 2,
        out_shape=[BLOCKS, SENT],
        scratch_shapes=[
            pltpu.VMEM((CHUNKS, ROWS, BLK), F32),
            pltpu.VMEM(BLOCKS.shape, BF16),
            pltpu.VMEM((CHUNKS, LEVELS, BLK, RANK), BF16),
            pltpu.VMEM((HALF, ROWS, 2 * RANK), F32),
            pltpu.VMEM(SENT.shape, BF16),
            pltpu.SemaphoreType.DMA((3, CHUNKS)),
            pltpu.SemaphoreType.DMA((HALF,)),
        ],
    )(in_hbm(field), in_hbm(far_basis))


LOWER, UPPER = pl.ds(0, PART), pl.ds(PART, PART)


def lower_kernel(place_ref, got_ref, back_hbm, up_hbm, low_ref, up_ref, sems):
    total = got_ref[0, UPPER, :].astype(F32)
    for k in range(1, GROUP):
        total += got_ref[k, UPPER, :].astype(F32)
    total = total.astype(BF16)
    for k in range(GROUP):
        up_ref[k] = total
    up_copy = pltpu.make_async_copy(up_ref, up_hbm, sems.at[0])
    up_copy.start()
    level = place_ref[0] // QUARTERS
    width = 1
    sums = [got_ref[k, LOWER, :].astype(F32) for k in range(GROUP)]
    while width < GROUP:
        sums = [sums[2 * k] + sums[2 * k + 1] for k in range(len(sums) // 2)]
        width *= 2
        own_level = width.bit_length() - 2

        @pl.when(level == own_level)
        def _(sums=sums, width=width, own_level=own_level):
            for k in range(GROUP):
                low_ref[k] = (sums[k // width] * gain(own_level)).astype(BF16)

    low_copy = pltpu.make_async_copy(low_ref, back_hbm.at[:, LOWER, :], sems.at[1])
    low_copy.start()
    up_copy.wait()
    low_copy.wait()


def lower_sums(place, got):
    part = (GROUP, PART, RANK)
    return call(
        lower_kernel,
        "lower_sums",
        in_specs=[SCALARS, IN_VMEM],
        out_specs=[IN_HBM] * 2,
        out_shape=[SENT, pltpu.HBM(part, BF16)],
        scratch_shapes=[
            pltpu.VMEM(part, BF16),
            pltpu.VMEM(part, BF16),
            pltpu.SemaphoreType.DMA((2,)),
        ],
    )(place, in_vmem(got))


def upper_kernel(place_ref, got_ref, _, back_hbm, up_ref, sem):
    level = place_ref[0] // QUARTERS
    shift = level + 1
    own = lax.shift_right_logical(place_ref[1], shift)
    total = jnp.zeros((PART, RANK), F32)
    for k in range(GROUP):
        same = (lax.shift_right_logical(jnp.int32(k), shift) == own).astype(F32)
        total += got_ref[k].astype(F32) * same
    scale = jnp.float32(gain(HALF))
    for other in range(1, HALF):
        scale = jnp.where(level == other, jnp.float32(gain(HALF + other)), scale)
    total = (total * scale).astype(BF16)
    for k in range(GROUP):
        up_ref[k] = total
    copy = pltpu.make_async_copy(up_ref, back_hbm.at[:, UPPER, :], sem.at[0])
    copy.start()
    copy.wait()


def upper_sums(place, got, back):
    return call(
        upper_kernel,
        "upper_sums",
        in_specs=[SCALARS, IN_VMEM, IN_HBM],
        out_specs=IN_HBM,
        out_shape=SENT,
        input_output_aliases={2: 0},
        scratch_shapes=[
            pltpu.VMEM((GROUP, PART, RANK), BF16),
            pltpu.SemaphoreType.DMA((1,)),
        ],
    )(place, in_vmem(got), in_hbm(back))


def near_kernel_body(slots_ref, left_hbm, own_hbm, right_hbm, kernel_hbm, *rest):
    out_hbm, ext_ref, kernel_ref, out_ref, ext_sems, kernel_sems, out_sems = rest[-7:]
    count = kernel_ref.shape[1]

    def side_copy(place, source):
        copy = pltpu.make_async_copy(
            source, ext_ref.at[pl.ds(place * CHUNKS, CHUNKS)], ext_sems.at[place]
        )
        copy.start()
        return copy

    own_copy = side_copy(1, own_hbm)
    order = [(block, 0) for block in range(CHUNKS)]
    order += [(block, k) for block in range(CHUNKS) for k in range(1, count)]
    kernels = {}

    def fetch(place):
        if place < len(order):
            block, k = order[place]
            kernels[block, k] = pltpu.make_async_copy(
                kernel_hbm.at[block, k], kernel_ref.at[block, k], kernel_sems.at[block, k]
            )
            kernels[block, k].start()

    for place in range(IN_FLIGHT):
        fetch(place)
    side_copies = [side_copy(0, left_hbm), side_copy(2, right_hbm)]

    def product(block, k, slot):
        kernels[block, k].wait()
        fetch(order.index((block, k)) + IN_FLIGHT)
        return lax.dot_general(
            ext_ref[slot], kernel_ref[block, k], NT, preferred_element_type=F32
        )

    own_copy.wait()
    for block in range(CHUNKS):
        total = product(block, 0, CHUNKS + block)
        if len(rest) > 7:
            approach_ref, gap_ref = rest[:2]
            square = (LOADS, LOADS)
            diagonal = lax.broadcasted_iota(jnp.int32, square, 0) == lax.broadcasted_iota(
                jnp.int32, square, 1
            )
            gaps = gap_ref[0:COMP, pl.ds(block * BLK, BLK)]
            for comp in range(COMP):
                rows = slice(comp * LOADS, (comp + 1) * LOADS)
                row = jnp.broadcast_to(approach_ref[comp : comp + 1, :], square)
                column = jnp.sum(jnp.where(diagonal, row, 0.0), axis=1, keepdims=True)
                out_ref[block, rows, :] = total[rows] - (column - gaps[comp : comp + 1])
        else:
            out_ref[block] = total
    for copy in side_copies:
        copy.wait()
    leaving = []
    for block in range(CHUNKS):
        total = out_ref[block]
        for k in range(1, count):
            slot = slots_ref[block, k] - slots_ref[block, 0] + (block + CHUNKS)
            total += product(block, k, slot)
        out_ref[block] = total
        copy = pltpu.make_async_copy(
            out_ref.at[block], out_hbm.at[:, pl.ds(block * BLK, BLK)], out_sems.at[block]
        )
        copy.start()
        leaving.append(copy)
    for copy in leaving:
        copy.wait()


def near_field(neighbours, left, own, right, near_kernel, *target):
    return call(
        near_kernel_body,
        "near_field",
        in_specs=[SCALARS] + [IN_HBM] * 4 + [IN_VMEM] * len(target),
        out_specs=IN_HBM,
        out_shape=FIELD,
        scratch_shapes=[
            pltpu.VMEM((3 * CHUNKS, ROWS, BLK), BF16),
            pltpu.VMEM(near_kernel.shape, BF16),
            pltpu.VMEM((CHUNKS, ROWS, BLK), F32),
            pltpu.SemaphoreType.DMA((3,)),
            pltpu.SemaphoreType.DMA(near_kernel.shape[:2]),
            pltpu.SemaphoreType.DMA((CHUNKS,)),
        ],
    )(neighbours, *map(in_hbm, (left, own, right, near_kernel)), *target)


def unpack(got_ref, coef_ref):
    for level in range(HALF):
        for quarter in range(QUARTERS):
            rows = pl.ds(quarter * PART, PART)
            slot = level * QUARTERS + quarter
            coef_ref[rows, level * RANK : (level + 1) * RANK] = got_ref[slot, 0:PART, :]
            coef_ref[rows, (HALF + level) * RANK : (HALF + level + 1) * RANK] = got_ref[
                slot, PART : 2 * PART, :
            ]


def far_field(coef_ref, basis_ref):
    basis = jnp.concatenate([basis_ref[level] for level in range(LEVELS)], axis=1)
    return lax.dot_general(coef_ref[...], basis, NT, preferred_element_type=F32)


COEFS = pltpu.VMEM((ROWS, LEVELS * RANK), BF16)


def start_chunks(source_hbm, ref, sems, row):
    copies = []
    for chunk in range(CHUNKS):
        copy = pltpu.make_async_copy(
            source_hbm.at[:, pl.ds(chunk * BLK, BLK)], ref.at[chunk], sems.at[row, chunk]
        )
        copy.start()
        copies.append(copy)
    return copies


def residual_kernel(got_ref, near_hbm, basis_ref, out_hbm, low_hbm, sent_hbm, *scratch):
    near_ref, out_ref, low_ref, sent_ref, coef_ref, sems, sent_sems = scratch
    arriving = start_chunks(near_hbm, near_ref, sems, 0)
    leaving = []
    unpack(got_ref, coef_ref)
    for chunk in range(CHUNKS):
        panels = pl.ds(chunk * BLK, BLK)
        out_ref[chunk] = far_field(coef_ref, basis_ref.at[:, panels, :])
    for chunk in range(CHUNKS):
        panels = pl.ds(chunk * BLK, BLK)
        arriving[chunk].wait()
        residual = out_ref[chunk] + near_ref[chunk]
        out_ref[chunk] = residual
        low_ref[chunk] = residual.astype(BF16)
        for copy in (
            pltpu.make_async_copy(out_ref.at[chunk], out_hbm.at[:, panels], sems.at[1, chunk]),
            pltpu.make_async_copy(low_ref.at[chunk], low_hbm.at[chunk], sems.at[2, chunk]),
        ):
            copy.start()
            leaving.append(copy)
    values = jnp.concatenate([low_ref[chunk] for chunk in range(CHUNKS)], axis=1)
    for level in range(HALF):
        pair = jnp.concatenate([basis_ref[level], basis_ref[HALF + level]], axis=1)
        coefs = jnp.dot(values, pair, preferred_element_type=F32)
        leaving.append(send_coefs(level, coefs, sent_ref, sent_hbm, sent_sems.at[level]))
    for copy in leaving:
        copy.wait()


def residual_step(got, near, far_basis):
    return call(
        residual_kernel,
        "residual",
        in_specs=[IN_VMEM, IN_HBM, IN_VMEM],
        out_specs=[IN_HBM] * 3,
        out_shape=[FIELD, BLOCKS, SENT],
        scratch_shapes=[
            pltpu.VMEM((CHUNKS, ROWS, BLK), F32),
            pltpu.VMEM((CHUNKS, ROWS, BLK), F32),
            pltpu.VMEM(BLOCKS.shape, BF16),
            pltpu.VMEM(SENT.shape, BF16),
            COEFS,
            pltpu.SemaphoreType.DMA((3, CHUNKS)),
            pltpu.SemaphoreType.DMA((HALF,)),
        ],
    )(in_vmem(got), in_hbm(near), in_vmem(far_basis))


def product_kernel(got_ref, near_hbm, residual_hbm, basis_ref, sums_ref, *scratch):
    near_ref, residual_ref, far_ref, coef_ref, sems = scratch
    nears = start_chunks(near_hbm, near_ref, sems, 0)
    residuals = start_chunks(residual_hbm, residual_ref, sems, 1)
    unpack(got_ref, coef_ref)
    totals = [jnp.zeros((LOADS, 128), F32)] * 2
    for chunk in range(CHUNKS):
        far_ref[chunk] = far_field(coef_ref, basis_ref.at[:, pl.ds(chunk * BLK, BLK), :])
    for chunk in range(CHUNKS):
        nears[chunk].wait()
        residuals[chunk].wait()
        image = far_ref[chunk] + near_ref[chunk]
        for place, product in enumerate((residual_ref[chunk] * image, image * image)):
            by_load = product[0:LOADS] + product[LOADS : 2 * LOADS] + product[2 * LOADS : ROWS]
            for lane in range(0, BLK, 128):
                totals[place] += by_load[:, lane : lane + 128]
    sums_ref[...] = jnp.sum(jnp.concatenate(totals, axis=0).T, axis=0, keepdims=True)


def local_products(got, near, residual, far_basis):
    return call(
        product_kernel,
        "products",
        in_specs=[IN_VMEM, IN_HBM, IN_HBM, IN_VMEM],
        out_specs=IN_VMEM,
        out_shape=SUMS,
        scratch_shapes=[
            pltpu.VMEM((CHUNKS, ROWS, BLK), F32),
            pltpu.VMEM((CHUNKS, ROWS, BLK), F32),
            pltpu.VMEM((CHUNKS, ROWS, BLK), F32),
            COEFS,
            pltpu.SemaphoreType.DMA((2, CHUNKS)),
        ],
    )(in_vmem(got), in_hbm(near), in_hbm(residual), in_vmem(far_basis))


def sort_kernel(order_ref, values_ref, out_ref):
    rows, cols = values_ref.shape[1], order_ref.shape[1]
    local = lax.rem(order_ref[...], PAN)
    chosen = lax.broadcasted_iota(jnp.int32, (rows, cols), 0) == local
    matrix = jnp.where(chosen, 1.0, 0.0).astype(BF16)
    left_over = values_ref[...]
    pieces = []
    for _ in range(3):
        pieces.append(left_over.astype(BF16).astype(F32))
        left_over = left_over - pieces[-1]
    pieces = jnp.concatenate(pieces, axis=0).astype(BF16)
    moved = jnp.dot(pieces, matrix, preferred_element_type=F32)
    count = out_ref.shape[0]
    out_ref[...] = (moved[:count] + moved[count : 2 * count]) + moved[2 * count :]


def sort_panels(order, values):
    return call(
        sort_kernel,
        "sort_panels",
        grid=(CHUNKS,),
        in_specs=[pl.BlockSpec((1, BLK), lambda b: (0, b)), whole(values.shape)],
        out_specs=PANEL_ROWS,
        out_shape=pltpu.HBM(values.shape, F32),
    )(order, values)


def final_kernel(entries, got_ref, field_ref, residual_ref, sorted_ref, out_hbm, *rest):
    step_ref, out_ref, sems = rest
    sums = jnp.sum(got_ref[...], axis=0) * (1.0 / entries)
    sums = jnp.broadcast_to(sums, (8, 2 * LOADS))
    square = jnp.concatenate([sums[:, LOADS:], sums[:, LOADS:]], axis=1)
    steps = sums / (square + 1e-06)
    step_ref[...] = steps[0, 0:LOADS]
    column = jnp.concatenate([steps] * 16, axis=0).T[0:LOADS, 0:1]
    comps = [slice(c * LOADS, (c + 1) * LOADS) for c in range(COMP)]
    leaving = []
    for chunk in range(CHUNKS):
        panels = pl.ds(chunk * BLK, BLK)
        normal, slide_a, slide_b = (
            field_ref[rows, panels] - column * residual_ref[rows, panels] for rows in comps
        )
        coeff = sorted_ref[3:4, panels]
        live = sorted_ref[4:5, panels]
        slip = jnp.sqrt(slide_a * slide_a + slide_b * slide_b + SLIP_EPS)
        stick = slip <= coeff * normal
        slid = jnp.maximum((normal + coeff * slip) / (1.0 + coeff * coeff), 0.0)
        pressed = jnp.where(stick, normal, slid)
        factor = jnp.where(stick, jnp.ones_like(slip), coeff * pressed / slip)
        out_ref[chunk, comps[0], :] = pressed * live
        out_ref[chunk, comps[1], :] = factor * slide_a * live
        out_ref[chunk, comps[2], :] = factor * slide_b * live
        copy = pltpu.make_async_copy(out_ref.at[chunk], out_hbm.at[:, panels], sems.at[chunk])
        copy.start()
        leaving.append(copy)
    for copy in leaving:
        copy.wait()


def final_step(got, field, residual, panel_rows, entries):
    return call(
        functools.partial(final_kernel, entries),
        "final",
        in_specs=[IN_VMEM] * 4,
        out_specs=[IN_HBM, IN_VMEM],
        out_shape=[FIELD, jax.ShapeDtypeStruct((LOADS,), F32)],
        scratch_shapes=[
            pltpu.VMEM((CHUNKS, ROWS, BLK), F32),
            pltpu.SemaphoreType.DMA((CHUNKS,)),
        ],
    )(in_vmem(got), in_vmem(field), in_vmem(residual), in_vmem(panel_rows))


def swap(blocks, axes):
    return lax.all_to_all(blocks, axes, 0, 0)


def beside(blocks):
    size = lax.axis_size(WIDE_NARROW)
    up = [(i, i + 1) for i in range(size - 1)]
    down = [(b, a) for a, b in up]
    return lax.ppermute(blocks, WIDE_NARROW, up), lax.ppermute(blocks, WIDE_NARROW, down)


def operator(place, low, sent, *early):
    sides = beside(low)
    lower, up = lower_sums(place, swap(sent, NARROW))
    upper, sides, early = lax.optimization_barrier((swap(up, WIDE), sides, early))
    return sides, swap(upper_sums(place, upper, lower), NARROW), early


def body(
    traction,
    near_kernel,
    neighbours,
    far_basis,
    surface_gap,
    friction,
    contact_flags,
    cluster_order,
    approach,
):
    field = traction.reshape(ROWS, PAN)
    place = jnp.stack([lax.axis_index(NARROW), lax.axis_index(WIDE)]).astype(jnp.int32)
    panel_rows = jnp.concatenate(
        [
            surface_gap,
            friction[None],
            contact_flags.astype(F32)[None],
            jnp.zeros((3, PAN), F32),
        ]
    )
    panel_rows = sort_panels(cluster_order[None], panel_rows)

    low, sent = first_coefs(field, far_basis)
    (left, right), coefs, (panel_rows,) = operator(place, low, sent, panel_rows)
    near = near_field(
        neighbours, left, low, right, near_kernel, approach, in_hbm(panel_rows)
    )
    residual, low, sent = residual_step(coefs, near, far_basis)
    (left, right), coefs, _ = operator(place, low, sent)
    near = near_field(neighbours, left, low, right, near_kernel)
    sums = local_products(coefs, near, residual, far_basis)

    devices = lax.axis_size(WIDE_NARROW)
    sums = swap(jnp.broadcast_to(sums[None], (devices, 1, 2 * LOADS)), WIDE_NARROW)
    entries = COMP * PAN * devices
    updated, steps = final_step(sums, field, residual, panel_rows, entries)
    shape = (COMP, LOADS, PAN)
    return updated.reshape(shape), residual.reshape(shape), steps


def solution(mesh):
    finer = Mesh(mesh.devices.reshape(8, 2, 4, 4), ("wide_0", "wide_1", "narrow_0", "narrow_1"))
    placed = (
        P(None, None, WIDE_NARROW),
        P(WIDE_NARROW, None, None, None),
        P(WIDE_NARROW, None),
        P(None, WIDE_NARROW, None),
        P(None, WIDE_NARROW),
        P(WIDE_NARROW),
        P(WIDE_NARROW),
        P(WIDE_NARROW),
        P(),
    )
    return jax.shard_map(
        body,
        mesh=finer,
        in_specs=placed,
        out_specs=(P(None, None, WIDE_NARROW), P(None, None, WIDE_NARROW), P()),
        check_vma=False,
    )
```

```python
import functools
import math

import jax
import jax.numpy as jnp
from jax import lax
from jax.experimental import pallas as pl
from jax.experimental.pallas import tpu as pltpu
from jax.sharding import Mesh
from jax.sharding import PartitionSpec as P

WIDE_NARROW = ("wide_0", "wide_1", "narrow_0", "narrow_1")
NARROW = ("narrow_0", "narrow_1")
WIDE = ("wide_0", "wide_1")

SLIP_EPS = 0.01
COMP = 3
LOADS = 64
ROWS = COMP * LOADS
PAN = 1536
BLK = 512
CHUNKS = PAN // BLK
LEVELS = 8
HALF = LEVELS // 2
RANK = 128
GROUP = 16
QUARTERS = 4
PART = ROWS // QUARTERS

F32 = jnp.float32
BF16 = jnp.bfloat16
NT = (((1,), (1,)), ((), ()))
LIMIT = 16 * 2**20
IN_FLIGHT = 5


def gain(level):
    return 0.64 / math.sqrt(RANK * PAN * 2 ** (level + 1))


def call(kernel, name, **kw):
    return pl.pallas_call(
        kernel,
        name=name,
        compiler_params=pltpu.CompilerParams(vmem_limit_bytes=LIMIT),
        **kw,
    )


def in_vmem(array):
    return pltpu.with_memory_space_constraint(array, pltpu.VMEM)


def in_hbm(array):
    return pltpu.with_memory_space_constraint(array, pltpu.HBM)


def whole(shape):
    return pl.BlockSpec(shape, lambda *_: (0,) * len(shape))


SCALARS = pl.BlockSpec(memory_space=pltpu.SMEM)
IN_VMEM = pl.BlockSpec(memory_space=pltpu.VMEM)
IN_HBM = pl.BlockSpec(memory_space=pltpu.HBM)
CHUNK = pl.BlockSpec((ROWS, BLK), lambda b: (0, b))
PANEL_ROWS = pl.BlockSpec((8, BLK), lambda b: (0, b))


def send_coefs(level, coefs, sent_ref, sent_hbm, sem):
    coefs = coefs.astype(BF16)
    for quarter in range(QUARTERS):
        rows = slice(quarter * PART, (quarter + 1) * PART)
        slot = level * QUARTERS + quarter
        sent_ref[slot, 0:PART, :] = coefs[rows, 0:RANK]
        sent_ref[slot, PART : 2 * PART, :] = coefs[rows, RANK : 2 * RANK]
    slots = pl.ds(level * QUARTERS, QUARTERS)
    copy = pltpu.make_async_copy(sent_ref.at[slots], sent_hbm.at[slots], sem)
    copy.start()
    return copy


def coef_kernel(field_hbm, basis_hbm, low_hbm, sent_hbm, *scratch):
    field_ref, low_ref, basis_ref, acc_ref, sent_ref, sems, sent_sems = scratch
    arriving, leaving = [], []
    for chunk in range(CHUNKS):
        panels = pl.ds(chunk * BLK, BLK)
        arriving.append(
            (
                pltpu.make_async_copy(
                    field_hbm.at[:, panels], field_ref.at[chunk], sems.at[0, chunk]
                ),
                pltpu.make_async_copy(
                    basis_hbm.at[:, panels, :], basis_ref.at[chunk], sems.at[1, chunk]
                ),
            )
        )
        for copy in arriving[-1]:
            copy.start()
    for chunk in range(CHUNKS):
        for copy in arriving[chunk]:
            copy.wait()
        values = field_ref[chunk].astype(BF16)
        low_ref[chunk] = values
        copy = pltpu.make_async_copy(low_ref.at[chunk], low_hbm.at[chunk], sems.at[2, chunk])
        copy.start()
        leaving.append(copy)
        for level in range(HALF):
            pair = jnp.concatenate(
                [basis_ref[chunk, level], basis_ref[chunk, HALF + level]], axis=1
            )
            part = jnp.dot(values, pair, preferred_element_type=F32)
            if chunk > 0:
                part += acc_ref[level]
            if chunk < CHUNKS - 1:
                acc_ref[level] = part
            else:
                leaving.append(send_coefs(level, part, sent_ref, sent_hbm, sent_sems.at[level]))
    for copy in leaving:
        copy.wait()


SENT = pltpu.HBM((GROUP, 2 * PART, RANK), BF16)
BLOCKS = pltpu.HBM((CHUNKS, ROWS, BLK), BF16)
FIELD = pltpu.HBM((ROWS, PAN), F32)
SUMS = jax.ShapeDtypeStruct((1, 2 * LOADS), F32)


def first_coefs(field, far_basis):
    return call(
        coef_kernel,
        "first_coefs",
        in_specs=[IN_HBM] * 2,
        out_specs=[IN_HBM] * 2,
        out_shape=[BLOCKS, SENT],
        scratch_shapes=[
            pltpu.VMEM((CHUNKS, ROWS, BLK), F32),
            pltpu.VMEM(BLOCKS.shape, BF16),
            pltpu.VMEM((CHUNKS, LEVELS, BLK, RANK), BF16),
            pltpu.VMEM((HALF, ROWS, 2 * RANK), F32),
            pltpu.VMEM(SENT.shape, BF16),
            pltpu.SemaphoreType.DMA((3, CHUNKS)),
            pltpu.SemaphoreType.DMA((HALF,)),
        ],
    )(in_hbm(field), in_hbm(far_basis))


LOWER, UPPER = pl.ds(0, PART), pl.ds(PART, PART)


def plane_kernel(got_ref, up_hbm, up_ref, sem):
    total = got_ref[0, UPPER, :].astype(F32)
    for k in range(1, GROUP):
        total += got_ref[k, UPPER, :].astype(F32)
    total = total.astype(BF16)
    for k in range(GROUP):
        up_ref[k] = total
    copy = pltpu.make_async_copy(up_ref, up_hbm, sem.at[0])
    copy.start()
    copy.wait()


def plane_sums(got):
    part = (GROUP, PART, RANK)
    return call(
        plane_kernel,
        "plane_sums",
        in_specs=[IN_VMEM],
        out_specs=IN_HBM,
        out_shape=pltpu.HBM(part, BF16),
        scratch_shapes=[pltpu.VMEM(part, BF16), pltpu.SemaphoreType.DMA((1,))],
    )(in_vmem(got))


def lower_kernel(place_ref, got_ref, back_hbm, low_ref, sem):
    level = place_ref[0] // QUARTERS
    width = 1
    sums = [got_ref[k, LOWER, :].astype(F32) for k in range(GROUP)]
    while width < GROUP:
        sums = [sums[2 * k] + sums[2 * k + 1] for k in range(len(sums) // 2)]
        width *= 2
        own_level = width.bit_length() - 2

        @pl.when(level == own_level)
        def _(sums=sums, width=width, own_level=own_level):
            for k in range(GROUP):
                low_ref[k] = (sums[k // width] * gain(own_level)).astype(BF16)

    copy = pltpu.make_async_copy(low_ref, back_hbm.at[:, LOWER, :], sem.at[0])
    copy.start()
    copy.wait()


def lower_sums(place, got):
    return call(
        lower_kernel,
        "lower_sums",
        in_specs=[SCALARS, IN_VMEM],
        out_specs=IN_HBM,
        out_shape=SENT,
        scratch_shapes=[
            pltpu.VMEM((GROUP, PART, RANK), BF16),
            pltpu.SemaphoreType.DMA((1,)),
        ],
    )(place, in_vmem(got))


def upper_kernel(place_ref, got_ref, _, back_hbm, up_ref, sem):
    level = place_ref[0] // QUARTERS
    shift = level + 1
    own = lax.shift_right_logical(place_ref[1], shift)
    total = jnp.zeros((PART, RANK), F32)
    for k in range(GROUP):
        same = (lax.shift_right_logical(jnp.int32(k), shift) == own).astype(F32)
        total += got_ref[k].astype(F32) * same
    scale = jnp.float32(gain(HALF))
    for other in range(1, HALF):
        scale = jnp.where(level == other, jnp.float32(gain(HALF + other)), scale)
    total = (total * scale).astype(BF16)
    for k in range(GROUP):
        up_ref[k] = total
    copy = pltpu.make_async_copy(up_ref, back_hbm.at[:, UPPER, :], sem.at[0])
    copy.start()
    copy.wait()


def upper_sums(place, got, back):
    return call(
        upper_kernel,
        "upper_sums",
        in_specs=[SCALARS, IN_VMEM, IN_HBM],
        out_specs=IN_HBM,
        out_shape=SENT,
        input_output_aliases={2: 0},
        scratch_shapes=[
            pltpu.VMEM((GROUP, PART, RANK), BF16),
            pltpu.SemaphoreType.DMA((1,)),
        ],
    )(place, in_vmem(got), in_hbm(back))


def near_kernel_body(slots_ref, left_hbm, own_hbm, right_hbm, kernel_hbm, *rest):
    out_hbm, ext_ref, kernel_ref, out_ref, ext_sems, kernel_sems, out_sems = rest[-7:]
    count = kernel_ref.shape[1]

    def side_copy(place, source):
        copy = pltpu.make_async_copy(
            source, ext_ref.at[pl.ds(place * CHUNKS, CHUNKS)], ext_sems.at[place]
        )
        copy.start()
        return copy

    own_copy = side_copy(1, own_hbm)
    order = [(block, 0) for block in range(CHUNKS)]
    order += [(block, k) for block in range(CHUNKS) for k in range(1, count)]
    kernels = {}

    def fetch(place):
        if place < len(order):
            block, k = order[place]
            kernels[block, k] = pltpu.make_async_copy(
                kernel_hbm.at[block, k], kernel_ref.at[block, k], kernel_sems.at[block, k]
            )
            kernels[block, k].start()

    for place in range(IN_FLIGHT):
        fetch(place)
    side_copies = [side_copy(0, left_hbm), side_copy(2, right_hbm)]

    def product(block, k, slot):
        kernels[block, k].wait()
        fetch(order.index((block, k)) + IN_FLIGHT)
        return lax.dot_general(
            ext_ref[slot], kernel_ref[block, k], NT, preferred_element_type=F32
        )

    own_copy.wait()
    for block in range(CHUNKS):
        total = product(block, 0, CHUNKS + block)
        if len(rest) > 7:
            approach_ref, gap_ref = rest[:2]
            square = (LOADS, LOADS)
            diagonal = lax.broadcasted_iota(jnp.int32, square, 0) == lax.broadcasted_iota(
                jnp.int32, square, 1
            )
            gaps = gap_ref[0:COMP, pl.ds(block * BLK, BLK)]
            for comp in range(COMP):
                rows = slice(comp * LOADS, (comp + 1) * LOADS)
                row = jnp.broadcast_to(approach_ref[comp : comp + 1, :], square)
                column = jnp.sum(jnp.where(diagonal, row, 0.0), axis=1, keepdims=True)
                out_ref[block, rows, :] = total[rows] - (column - gaps[comp : comp + 1])
        else:
            out_ref[block] = total
    for copy in side_copies:
        copy.wait()
    leaving = []
    for block in range(CHUNKS):
        total = out_ref[block]
        for k in range(1, count):
            slot = slots_ref[block, k] - slots_ref[block, 0] + (block + CHUNKS)
            total += product(block, k, slot)
        out_ref[block] = total
        copy = pltpu.make_async_copy(
            out_ref.at[block], out_hbm.at[:, pl.ds(block * BLK, BLK)], out_sems.at[block]
        )
        copy.start()
        leaving.append(copy)
    for copy in leaving:
        copy.wait()


def near_field(neighbours, left, own, right, near_kernel, *target):
    return call(
        near_kernel_body,
        "near_field",
        in_specs=[SCALARS] + [IN_HBM] * 4 + [IN_VMEM] * len(target),
        out_specs=IN_HBM,
        out_shape=FIELD,
        scratch_shapes=[
            pltpu.VMEM((3 * CHUNKS, ROWS, BLK), BF16),
            pltpu.VMEM(near_kernel.shape, BF16),
            pltpu.VMEM((CHUNKS, ROWS, BLK), F32),
            pltpu.SemaphoreType.DMA((3,)),
            pltpu.SemaphoreType.DMA(near_kernel.shape[:2]),
            pltpu.SemaphoreType.DMA((CHUNKS,)),
        ],
    )(neighbours, *map(in_hbm, (left, own, right, near_kernel)), *target)


def unpack(got_ref, coef_ref):
    for level in range(HALF):
        for quarter in range(QUARTERS):
            rows = pl.ds(quarter * PART, PART)
            slot = level * QUARTERS + quarter
            coef_ref[rows, level * RANK : (level + 1) * RANK] = got_ref[slot, 0:PART, :]
            coef_ref[rows, (HALF + level) * RANK : (HALF + level + 1) * RANK] = got_ref[
                slot, PART : 2 * PART, :
            ]


def far_field(coef_ref, basis_ref):
    basis = jnp.concatenate([basis_ref[level] for level in range(LEVELS)], axis=1)
    return lax.dot_general(coef_ref[...], basis, NT, preferred_element_type=F32)


COEFS = pltpu.VMEM((ROWS, LEVELS * RANK), BF16)


def start_chunks(source_hbm, ref, sems, row):
    copies = []
    for chunk in range(CHUNKS):
        copy = pltpu.make_async_copy(
            source_hbm.at[:, pl.ds(chunk * BLK, BLK)], ref.at[chunk], sems.at[row, chunk]
        )
        copy.start()
        copies.append(copy)
    return copies


def residual_kernel(got_ref, near_hbm, basis_ref, out_hbm, low_hbm, sent_hbm, *scratch):
    near_ref, out_ref, low_ref, sent_ref, coef_ref, sems, sent_sems = scratch
    arriving = start_chunks(near_hbm, near_ref, sems, 0)
    leaving = []
    unpack(got_ref, coef_ref)
    for chunk in range(CHUNKS):
        panels = pl.ds(chunk * BLK, BLK)
        out_ref[chunk] = far_field(coef_ref, basis_ref.at[:, panels, :])
    for chunk in range(CHUNKS):
        panels = pl.ds(chunk * BLK, BLK)
        arriving[chunk].wait()
        residual = out_ref[chunk] + near_ref[chunk]
        out_ref[chunk] = residual
        low_ref[chunk] = residual.astype(BF16)
        for copy in (
            pltpu.make_async_copy(out_ref.at[chunk], out_hbm.at[:, panels], sems.at[1, chunk]),
            pltpu.make_async_copy(low_ref.at[chunk], low_hbm.at[chunk], sems.at[2, chunk]),
        ):
            copy.start()
            leaving.append(copy)
    values = jnp.concatenate([low_ref[chunk] for chunk in range(CHUNKS)], axis=1)
    for level in range(HALF):
        pair = jnp.concatenate([basis_ref[level], basis_ref[HALF + level]], axis=1)
        coefs = jnp.dot(values, pair, preferred_element_type=F32)
        leaving.append(send_coefs(level, coefs, sent_ref, sent_hbm, sent_sems.at[level]))
    for copy in leaving:
        copy.wait()


def residual_step(got, near, far_basis):
    return call(
        residual_kernel,
        "residual",
        in_specs=[IN_VMEM, IN_HBM, IN_VMEM],
        out_specs=[IN_HBM] * 3,
        out_shape=[FIELD, BLOCKS, SENT],
        scratch_shapes=[
            pltpu.VMEM((CHUNKS, ROWS, BLK), F32),
            pltpu.VMEM((CHUNKS, ROWS, BLK), F32),
            pltpu.VMEM(BLOCKS.shape, BF16),
            pltpu.VMEM(SENT.shape, BF16),
            COEFS,
            pltpu.SemaphoreType.DMA((3, CHUNKS)),
            pltpu.SemaphoreType.DMA((HALF,)),
        ],
    )(in_vmem(got), in_hbm(near), in_vmem(far_basis))


def product_kernel(got_ref, near_hbm, residual_hbm, basis_ref, sums_ref, *scratch):
    near_ref, residual_ref, far_ref, coef_ref, sems = scratch
    nears = start_chunks(near_hbm, near_ref, sems, 0)
    residuals = start_chunks(residual_hbm, residual_ref, sems, 1)
    unpack(got_ref, coef_ref)
    totals = [jnp.zeros((LOADS, 128), F32)] * 2
    for chunk in range(CHUNKS):
        far_ref[chunk] = far_field(coef_ref, basis_ref.at[:, pl.ds(chunk * BLK, BLK), :])
    for chunk in range(CHUNKS):
        nears[chunk].wait()
        residuals[chunk].wait()
        image = far_ref[chunk] + near_ref[chunk]
        for place, product in enumerate((residual_ref[chunk] * image, image * image)):
            by_load = product[0:LOADS] + product[LOADS : 2 * LOADS] + product[2 * LOADS : ROWS]
            for lane in range(0, BLK, 128):
                totals[place] += by_load[:, lane : lane + 128]
    sums_ref[...] = jnp.sum(jnp.concatenate(totals, axis=0).T, axis=0, keepdims=True)


def local_products(got, near, residual, far_basis):
    return call(
        product_kernel,
        "products",
        in_specs=[IN_VMEM, IN_HBM, IN_HBM, IN_VMEM],
        out_specs=IN_VMEM,
        out_shape=SUMS,
        scratch_shapes=[
            pltpu.VMEM((CHUNKS, ROWS, BLK), F32),
            pltpu.VMEM((CHUNKS, ROWS, BLK), F32),
            pltpu.VMEM((CHUNKS, ROWS, BLK), F32),
            COEFS,
            pltpu.SemaphoreType.DMA((2, CHUNKS)),
        ],
    )(in_vmem(got), in_hbm(near), in_hbm(residual), in_vmem(far_basis))


def sort_kernel(order_ref, values_ref, out_ref):
    rows, cols = values_ref.shape[1], order_ref.shape[1]
    local = lax.rem(order_ref[...], PAN)
    chosen = lax.broadcasted_iota(jnp.int32, (rows, cols), 0) == local
    matrix = jnp.where(chosen, 1.0, 0.0).astype(BF16)
    left_over = values_ref[...]
    pieces = []
    for _ in range(3):
        pieces.append(left_over.astype(BF16).astype(F32))
        left_over = left_over - pieces[-1]
    pieces = jnp.concatenate(pieces, axis=0).astype(BF16)
    moved = jnp.dot(pieces, matrix, preferred_element_type=F32)
    count = out_ref.shape[0]
    out_ref[...] = (moved[:count] + moved[count : 2 * count]) + moved[2 * count :]


def sort_panels(order, values):
    return call(
        sort_kernel,
        "sort_panels",
        grid=(CHUNKS,),
        in_specs=[pl.BlockSpec((1, BLK), lambda b: (0, b)), whole(values.shape)],
        out_specs=PANEL_ROWS,
        out_shape=pltpu.HBM(values.shape, F32),
    )(order, values)


def final_kernel(entries, got_ref, field_ref, residual_ref, sorted_ref, out_hbm, *rest):
    step_ref, out_ref, sems = rest
    sums = jnp.sum(got_ref[...], axis=0) * (1.0 / entries)
    sums = jnp.broadcast_to(sums, (8, 2 * LOADS))
    square = jnp.concatenate([sums[:, LOADS:], sums[:, LOADS:]], axis=1)
    steps = sums / (square + 1e-06)
    step_ref[...] = steps[0, 0:LOADS]
    column = jnp.concatenate([steps] * 16, axis=0).T[0:LOADS, 0:1]
    comps = [slice(c * LOADS, (c + 1) * LOADS) for c in range(COMP)]
    leaving = []
    for chunk in range(CHUNKS):
        panels = pl.ds(chunk * BLK, BLK)
        normal, slide_a, slide_b = (
            field_ref[rows, panels] - column * residual_ref[rows, panels] for rows in comps
        )
        coeff = sorted_ref[3:4, panels]
        live = sorted_ref[4:5, panels]
        slip = jnp.sqrt(slide_a * slide_a + slide_b * slide_b + SLIP_EPS)
        stick = slip <= coeff * normal
        slid = jnp.maximum((normal + coeff * slip) / (1.0 + coeff * coeff), 0.0)
        pressed = jnp.where(stick, normal, slid)
        factor = jnp.where(stick, jnp.ones_like(slip), coeff * pressed / slip)
        out_ref[chunk, comps[0], :] = pressed * live
        out_ref[chunk, comps[1], :] = factor * slide_a * live
        out_ref[chunk, comps[2], :] = factor * slide_b * live
        copy = pltpu.make_async_copy(out_ref.at[chunk], out_hbm.at[:, panels], sems.at[chunk])
        copy.start()
        leaving.append(copy)
    for copy in leaving:
        copy.wait()


def final_step(got, field, residual, panel_rows, entries):
    return call(
        functools.partial(final_kernel, entries),
        "final",
        in_specs=[IN_VMEM] * 4,
        out_specs=[IN_HBM, IN_VMEM],
        out_shape=[FIELD, jax.ShapeDtypeStruct((LOADS,), F32)],
        scratch_shapes=[
            pltpu.VMEM((CHUNKS, ROWS, BLK), F32),
            pltpu.SemaphoreType.DMA((CHUNKS,)),
        ],
    )(in_vmem(got), in_vmem(field), in_vmem(residual), in_vmem(panel_rows))


def swap(blocks, axes):
    return lax.all_to_all(blocks, axes, 0, 0)


def beside(blocks):
    size = lax.axis_size(WIDE_NARROW)
    up = [(i, i + 1) for i in range(size - 1)]
    down = [(b, a) for a, b in up]
    return lax.ppermute(blocks, WIDE_NARROW, up), lax.ppermute(blocks, WIDE_NARROW, down)


def operator(place, low, sent, *early):
    sides = beside(low)
    got = swap(sent, NARROW)
    up = plane_sums(got)
    lower = lower_sums(place, got)
    upper, sides, early = lax.optimization_barrier((swap(up, WIDE), sides, early))
    return sides, swap(upper_sums(place, upper, lower), NARROW), early


def body(
    traction,
    near_kernel,
    neighbours,
    far_basis,
    surface_gap,
    friction,
    contact_flags,
    cluster_order,
    approach,
):
    field = traction.reshape(ROWS, PAN)
    place = jnp.stack([lax.axis_index(NARROW), lax.axis_index(WIDE)]).astype(jnp.int32)
    panel_rows = jnp.concatenate(
        [
            surface_gap,
            friction[None],
            contact_flags.astype(F32)[None],
            jnp.zeros((3, PAN), F32),
        ]
    )
    panel_rows = sort_panels(cluster_order[None], panel_rows)

    low, sent = first_coefs(field, far_basis)
    (left, right), coefs, (panel_rows,) = operator(place, low, sent, panel_rows)
    near = near_field(
        neighbours, left, low, right, near_kernel, approach, in_hbm(panel_rows)
    )
    residual, low, sent = residual_step(coefs, near, far_basis)
    (left, right), coefs, _ = operator(place, low, sent)
    near = near_field(neighbours, left, low, right, near_kernel)
    sums = local_products(coefs, near, residual, far_basis)

    devices = lax.axis_size(WIDE_NARROW)
    sums = swap(jnp.broadcast_to(sums[None], (devices, 1, 2 * LOADS)), WIDE_NARROW)
    entries = COMP * PAN * devices
    updated, steps = final_step(sums, field, residual, panel_rows, entries)
    shape = (COMP, LOADS, PAN)
    return updated.reshape(shape), residual.reshape(shape), steps


def solution(mesh):
    finer = Mesh(mesh.devices.reshape(8, 2, 4, 4), ("wide_0", "wide_1", "narrow_0", "narrow_1"))
    placed = (
        P(None, None, WIDE_NARROW),
        P(WIDE_NARROW, None, None, None),
        P(WIDE_NARROW, None),
        P(None, WIDE_NARROW, None),
        P(None, WIDE_NARROW),
        P(WIDE_NARROW),
        P(WIDE_NARROW),
        P(WIDE_NARROW),
        P(),
    )
    return jax.shard_map(
        body,
        mesh=finer,
        in_specs=placed,
        out_specs=(P(None, None, WIDE_NARROW), P(None, None, WIDE_NARROW), P()),
        check_vma=False,
    )
```

```python
import functools
import math

import jax
import jax.numpy as jnp
from jax import lax
from jax.experimental import pallas as pl
from jax.experimental.pallas import tpu as pltpu
from jax.sharding import Mesh
from jax.sharding import PartitionSpec as P

WIDE_NARROW = ("wide_0", "wide_1", "narrow_0", "narrow_1")
NARROW = ("narrow_0", "narrow_1")
WIDE = ("wide_0", "wide_1")

SLIP_EPS = 0.01
COMP = 3
LOADS = 64
ROWS = COMP * LOADS
PAN = 1536
BLK = 512
CHUNKS = PAN // BLK
PIECE = 256
PIECES = PAN // PIECE
LEVELS = 8
HALF = LEVELS // 2
RANK = 128
GROUP = 16
QUARTERS = 4
PART = ROWS // QUARTERS

F32 = jnp.float32
BF16 = jnp.bfloat16
NT = (((1,), (1,)), ((), ()))
LIMIT = 16 * 2**20
IN_FLIGHT = 5


def gain(level):
    return 0.64 / math.sqrt(RANK * PAN * 2 ** (level + 1))


def call(kernel, name, **kw):
    return pl.pallas_call(
        kernel,
        name=name,
        compiler_params=pltpu.CompilerParams(vmem_limit_bytes=LIMIT),
        **kw,
    )


def in_vmem(array):
    return pltpu.with_memory_space_constraint(array, pltpu.VMEM)


def in_hbm(array):
    return pltpu.with_memory_space_constraint(array, pltpu.HBM)


def whole(shape):
    return pl.BlockSpec(shape, lambda *_: (0,) * len(shape))


SCALARS = pl.BlockSpec(memory_space=pltpu.SMEM)
IN_VMEM = pl.BlockSpec(memory_space=pltpu.VMEM)
IN_HBM = pl.BlockSpec(memory_space=pltpu.HBM)
CHUNK = pl.BlockSpec((ROWS, BLK), lambda b: (0, b))
PANEL_ROWS = pl.BlockSpec((8, BLK), lambda b: (0, b))


def send_coefs(level, coefs, sent_ref, sent_hbm, sem):
    coefs = coefs.astype(BF16)
    for quarter in range(QUARTERS):
        rows = slice(quarter * PART, (quarter + 1) * PART)
        slot = level * QUARTERS + quarter
        sent_ref[slot, 0:PART, :] = coefs[rows, 0:RANK]
        sent_ref[slot, PART : 2 * PART, :] = coefs[rows, RANK : 2 * RANK]
    slots = pl.ds(level * QUARTERS, QUARTERS)
    copy = pltpu.make_async_copy(sent_ref.at[slots], sent_hbm.at[slots], sem)
    copy.start()
    return copy


def coef_kernel(field_hbm, basis_hbm, low_hbm, sent_hbm, *scratch):
    field_ref, low_ref, basis_ref, acc_ref, sent_ref, sems, sent_sems = scratch
    arriving, leaving = [], []
    for chunk in range(PIECES):
        panels = pl.ds(chunk * PIECE, PIECE)
        arriving.append(
            (
                pltpu.make_async_copy(
                    field_hbm.at[:, panels], field_ref.at[chunk], sems.at[0, chunk]
                ),
                pltpu.make_async_copy(
                    basis_hbm.at[:, panels, :], basis_ref.at[chunk], sems.at[1, chunk]
                ),
            )
        )
        for copy in arriving[-1]:
            copy.start()
    for chunk in range(PIECES):
        for copy in arriving[chunk]:
            copy.wait()
        values = field_ref[chunk].astype(BF16)
        block, start = divmod(chunk * PIECE, BLK)
        low_ref[block, :, start : start + PIECE] = values
        if start + PIECE == BLK:
            copy = pltpu.make_async_copy(low_ref.at[block], low_hbm.at[block], sems.at[2, block])
            copy.start()
            leaving.append(copy)
        for level in range(HALF):
            pair = jnp.concatenate(
                [basis_ref[chunk, level], basis_ref[chunk, HALF + level]], axis=1
            )
            part = jnp.dot(values, pair, preferred_element_type=F32)
            if chunk > 0:
                part += acc_ref[level]
            if chunk < PIECES - 1:
                acc_ref[level] = part
            else:
                leaving.append(send_coefs(level, part, sent_ref, sent_hbm, sent_sems.at[level]))
    for copy in leaving:
        copy.wait()


SENT = pltpu.HBM((GROUP, 2 * PART, RANK), BF16)
BLOCKS = pltpu.HBM((CHUNKS, ROWS, BLK), BF16)
FIELD = pltpu.HBM((ROWS, PAN), F32)
SUMS = jax.ShapeDtypeStruct((1, 2 * LOADS), F32)


def first_coefs(field, far_basis):
    return call(
        coef_kernel,
        "first_coefs",
        in_specs=[IN_HBM] * 2,
        out_specs=[IN_HBM] * 2,
        out_shape=[BLOCKS, SENT],
        scratch_shapes=[
            pltpu.VMEM((PIECES, ROWS, PIECE), F32),
            pltpu.VMEM(BLOCKS.shape, BF16),
            pltpu.VMEM((PIECES, LEVELS, PIECE, RANK), BF16),
            pltpu.VMEM((HALF, ROWS, 2 * RANK), F32),
            pltpu.VMEM(SENT.shape, BF16),
            pltpu.SemaphoreType.DMA((3, PIECES)),
            pltpu.SemaphoreType.DMA((HALF,)),
        ],
    )(in_hbm(field), in_hbm(far_basis))


LOWER, UPPER = pl.ds(0, PART), pl.ds(PART, PART)


def plane_kernel(got_ref, up_hbm, up_ref, sem):
    total = got_ref[0, UPPER, :].astype(F32)
    for k in range(1, GROUP):
        total += got_ref[k, UPPER, :].astype(F32)
    total = total.astype(BF16)
    for k in range(GROUP):
        up_ref[k] = total
    copy = pltpu.make_async_copy(up_ref, up_hbm, sem.at[0])
    copy.start()
    copy.wait()


def plane_sums(got):
    part = (GROUP, PART, RANK)
    return call(
        plane_kernel,
        "plane_sums",
        in_specs=[IN_VMEM],
        out_specs=IN_HBM,
        out_shape=pltpu.HBM(part, BF16),
        scratch_shapes=[pltpu.VMEM(part, BF16), pltpu.SemaphoreType.DMA((1,))],
    )(in_vmem(got))


def lower_kernel(place_ref, got_ref, back_hbm, low_ref, sem):
    level = place_ref[0] // QUARTERS
    width = 1
    sums = [got_ref[k, LOWER, :].astype(F32) for k in range(GROUP)]
    while width < GROUP:
        sums = [sums[2 * k] + sums[2 * k + 1] for k in range(len(sums) // 2)]
        width *= 2
        own_level = width.bit_length() - 2

        @pl.when(level == own_level)
        def _(sums=sums, width=width, own_level=own_level):
            for k in range(GROUP):
                low_ref[k] = (sums[k // width] * gain(own_level)).astype(BF16)

    copy = pltpu.make_async_copy(low_ref, back_hbm.at[:, LOWER, :], sem.at[0])
    copy.start()
    copy.wait()


def lower_sums(place, got):
    return call(
        lower_kernel,
        "lower_sums",
        in_specs=[SCALARS, IN_VMEM],
        out_specs=IN_HBM,
        out_shape=SENT,
        scratch_shapes=[
            pltpu.VMEM((GROUP, PART, RANK), BF16),
            pltpu.SemaphoreType.DMA((1,)),
        ],
    )(place, in_vmem(got))


def upper_kernel(place_ref, got_ref, _, back_hbm, up_ref, sem):
    level = place_ref[0] // QUARTERS
    shift = level + 1
    own = lax.shift_right_logical(place_ref[1], shift)
    total = jnp.zeros((PART, RANK), F32)
    for k in range(GROUP):
        same = (lax.shift_right_logical(jnp.int32(k), shift) == own).astype(F32)
        total += got_ref[k].astype(F32) * same
    scale = jnp.float32(gain(HALF))
    for other in range(1, HALF):
        scale = jnp.where(level == other, jnp.float32(gain(HALF + other)), scale)
    total = (total * scale).astype(BF16)
    for k in range(GROUP):
        up_ref[k] = total
    copy = pltpu.make_async_copy(up_ref, back_hbm.at[:, UPPER, :], sem.at[0])
    copy.start()
    copy.wait()


def upper_sums(place, got, back):
    return call(
        upper_kernel,
        "upper_sums",
        in_specs=[SCALARS, IN_VMEM, IN_HBM],
        out_specs=IN_HBM,
        out_shape=SENT,
        input_output_aliases={2: 0},
        scratch_shapes=[
            pltpu.VMEM((GROUP, PART, RANK), BF16),
            pltpu.SemaphoreType.DMA((1,)),
        ],
    )(place, in_vmem(got), in_hbm(back))


def near_kernel_body(slots_ref, left_hbm, own_hbm, right_hbm, kernel_hbm, *rest):
    out_hbm, ext_ref, kernel_ref, out_ref, ext_sems, kernel_sems, out_sems = rest[-7:]
    count = kernel_ref.shape[1]

    def side_copy(place, source):
        copy = pltpu.make_async_copy(
            source, ext_ref.at[pl.ds(place * CHUNKS, CHUNKS)], ext_sems.at[place]
        )
        copy.start()
        return copy

    own_copy = side_copy(1, own_hbm)
    order = [(block, 0) for block in range(CHUNKS)]
    order += [(block, k) for block in range(CHUNKS) for k in range(1, count)]
    kernels = {}

    def fetch(place):
        if place < len(order):
            block, k = order[place]
            kernels[block, k] = pltpu.make_async_copy(
                kernel_hbm.at[block, k], kernel_ref.at[block, k], kernel_sems.at[block, k]
            )
            kernels[block, k].start()

    for place in range(IN_FLIGHT):
        fetch(place)
    side_copies = [side_copy(0, left_hbm), side_copy(2, right_hbm)]

    def product(block, k, slot):
        kernels[block, k].wait()
        fetch(order.index((block, k)) + IN_FLIGHT)
        return lax.dot_general(
            ext_ref[slot], kernel_ref[block, k], NT, preferred_element_type=F32
        )

    own_copy.wait()
    for block in range(CHUNKS):
        total = product(block, 0, CHUNKS + block)
        if len(rest) > 7:
            approach_ref, gap_ref = rest[:2]
            square = (LOADS, LOADS)
            diagonal = lax.broadcasted_iota(jnp.int32, square, 0) == lax.broadcasted_iota(
                jnp.int32, square, 1
            )
            gaps = gap_ref[0:COMP, pl.ds(block * BLK, BLK)]
            for comp in range(COMP):
                rows = slice(comp * LOADS, (comp + 1) * LOADS)
                row = jnp.broadcast_to(approach_ref[comp : comp + 1, :], square)
                column = jnp.sum(jnp.where(diagonal, row, 0.0), axis=1, keepdims=True)
                out_ref[block, rows, :] = total[rows] - (column - gaps[comp : comp + 1])
        else:
            out_ref[block] = total
    for copy in side_copies:
        copy.wait()
    leaving = []
    for block in range(CHUNKS):
        total = out_ref[block]
        for k in range(1, count):
            slot = slots_ref[block, k] - slots_ref[block, 0] + (block + CHUNKS)
            total += product(block, k, slot)
        out_ref[block] = total
        copy = pltpu.make_async_copy(
            out_ref.at[block], out_hbm.at[:, pl.ds(block * BLK, BLK)], out_sems.at[block]
        )
        copy.start()
        leaving.append(copy)
    for copy in leaving:
        copy.wait()


def near_field(neighbours, left, own, right, near_kernel, *target):
    return call(
        near_kernel_body,
        "near_field",
        in_specs=[SCALARS] + [IN_HBM] * 4 + [IN_VMEM] * len(target),
        out_specs=IN_HBM,
        out_shape=FIELD,
        scratch_shapes=[
            pltpu.VMEM((3 * CHUNKS, ROWS, BLK), BF16),
            pltpu.VMEM(near_kernel.shape, BF16),
            pltpu.VMEM((CHUNKS, ROWS, BLK), F32),
            pltpu.SemaphoreType.DMA((3,)),
            pltpu.SemaphoreType.DMA(near_kernel.shape[:2]),
            pltpu.SemaphoreType.DMA((CHUNKS,)),
        ],
    )(neighbours, *map(in_hbm, (left, own, right, near_kernel)), *target)


def unpack(got_ref, coef_ref):
    for level in range(HALF):
        for quarter in range(QUARTERS):
            rows = pl.ds(quarter * PART, PART)
            slot = level * QUARTERS + quarter
            coef_ref[rows, level * RANK : (level + 1) * RANK] = got_ref[slot, 0:PART, :]
            coef_ref[rows, (HALF + level) * RANK : (HALF + level + 1) * RANK] = got_ref[
                slot, PART : 2 * PART, :
            ]


def far_field(coef_ref, basis_ref):
    basis = jnp.concatenate([basis_ref[level] for level in range(LEVELS)], axis=1)
    return lax.dot_general(coef_ref[...], basis, NT, preferred_element_type=F32)


COEFS = pltpu.VMEM((ROWS, LEVELS * RANK), BF16)


def start_chunks(source_hbm, ref, sems, row):
    copies = []
    for chunk in range(CHUNKS):
        copy = pltpu.make_async_copy(
            source_hbm.at[:, pl.ds(chunk * BLK, BLK)], ref.at[chunk], sems.at[row, chunk]
        )
        copy.start()
        copies.append(copy)
    return copies


def residual_kernel(got_ref, near_hbm, basis_ref, out_hbm, low_hbm, sent_hbm, *scratch):
    near_ref, out_ref, low_ref, sent_ref, coef_ref, sems, sent_sems = scratch
    arriving = start_chunks(near_hbm, near_ref, sems, 0)
    leaving = []
    unpack(got_ref, coef_ref)
    for chunk in range(CHUNKS):
        panels = pl.ds(chunk * BLK, BLK)
        out_ref[chunk] = far_field(coef_ref, basis_ref.at[:, panels, :])
    for chunk in range(CHUNKS):
        panels = pl.ds(chunk * BLK, BLK)
        arriving[chunk].wait()
        residual = out_ref[chunk] + near_ref[chunk]
        out_ref[chunk] = residual
        low_ref[chunk] = residual.astype(BF16)
        for copy in (
            pltpu.make_async_copy(out_ref.at[chunk], out_hbm.at[:, panels], sems.at[1, chunk]),
            pltpu.make_async_copy(low_ref.at[chunk], low_hbm.at[chunk], sems.at[2, chunk]),
        ):
            copy.start()
            leaving.append(copy)
    values = jnp.concatenate([low_ref[chunk] for chunk in range(CHUNKS)], axis=1)
    for level in range(HALF):
        pair = jnp.concatenate([basis_ref[level], basis_ref[HALF + level]], axis=1)
        coefs = jnp.dot(values, pair, preferred_element_type=F32)
        leaving.append(send_coefs(level, coefs, sent_ref, sent_hbm, sent_sems.at[level]))
    for copy in leaving:
        copy.wait()


def residual_step(got, near, far_basis):
    return call(
        residual_kernel,
        "residual",
        in_specs=[IN_VMEM, IN_HBM, IN_VMEM],
        out_specs=[IN_HBM] * 3,
        out_shape=[FIELD, BLOCKS, SENT],
        scratch_shapes=[
            pltpu.VMEM((CHUNKS, ROWS, BLK), F32),
            pltpu.VMEM((CHUNKS, ROWS, BLK), F32),
            pltpu.VMEM(BLOCKS.shape, BF16),
            pltpu.VMEM(SENT.shape, BF16),
            COEFS,
            pltpu.SemaphoreType.DMA((3, CHUNKS)),
            pltpu.SemaphoreType.DMA((HALF,)),
        ],
    )(in_vmem(got), in_hbm(near), in_vmem(far_basis))


def product_kernel(got_ref, near_hbm, residual_hbm, basis_ref, sums_ref, *scratch):
    near_ref, residual_ref, far_ref, coef_ref, sems = scratch
    nears = start_chunks(near_hbm, near_ref, sems, 0)
    residuals = start_chunks(residual_hbm, residual_ref, sems, 1)
    unpack(got_ref, coef_ref)
    totals = [jnp.zeros((LOADS, 128), F32)] * 2
    for chunk in range(CHUNKS):
        far_ref[chunk] = far_field(coef_ref, basis_ref.at[:, pl.ds(chunk * BLK, BLK), :])
    for chunk in range(CHUNKS):
        nears[chunk].wait()
        residuals[chunk].wait()
        image = far_ref[chunk] + near_ref[chunk]
        for place, product in enumerate((residual_ref[chunk] * image, image * image)):
            by_load = product[0:LOADS] + product[LOADS : 2 * LOADS] + product[2 * LOADS : ROWS]
            for lane in range(0, BLK, 128):
                totals[place] += by_load[:, lane : lane + 128]
    sums_ref[...] = jnp.sum(jnp.concatenate(totals, axis=0).T, axis=0, keepdims=True)


def local_products(got, near, residual, far_basis):
    return call(
        product_kernel,
        "products",
        in_specs=[IN_VMEM, IN_HBM, IN_HBM, IN_VMEM],
        out_specs=IN_VMEM,
        out_shape=SUMS,
        scratch_shapes=[
            pltpu.VMEM((CHUNKS, ROWS, BLK), F32),
            pltpu.VMEM((CHUNKS, ROWS, BLK), F32),
            pltpu.VMEM((CHUNKS, ROWS, BLK), F32),
            COEFS,
            pltpu.SemaphoreType.DMA((2, CHUNKS)),
        ],
    )(in_vmem(got), in_hbm(near), in_hbm(residual), in_vmem(far_basis))


def sort_kernel(order_ref, values_ref, out_ref):
    rows, cols = values_ref.shape[1], order_ref.shape[1]
    local = lax.rem(order_ref[...], PAN)
    chosen = lax.broadcasted_iota(jnp.int32, (rows, cols), 0) == local
    matrix = jnp.where(chosen, 1.0, 0.0).astype(BF16)
    left_over = values_ref[...]
    pieces = []
    for _ in range(3):
        pieces.append(left_over.astype(BF16).astype(F32))
        left_over = left_over - pieces[-1]
    pieces = jnp.concatenate(pieces, axis=0).astype(BF16)
    moved = jnp.dot(pieces, matrix, preferred_element_type=F32)
    count = out_ref.shape[0]
    out_ref[...] = (moved[:count] + moved[count : 2 * count]) + moved[2 * count :]


def sort_panels(order, values):
    return call(
        sort_kernel,
        "sort_panels",
        grid=(CHUNKS,),
        in_specs=[pl.BlockSpec((1, BLK), lambda b: (0, b)), whole(values.shape)],
        out_specs=PANEL_ROWS,
        out_shape=pltpu.HBM(values.shape, F32),
    )(order, values)


def final_kernel(entries, got_ref, field_ref, residual_ref, sorted_ref, out_hbm, *rest):
    step_ref, out_ref, sems = rest
    sums = jnp.sum(got_ref[...], axis=0) * (1.0 / entries)
    sums = jnp.broadcast_to(sums, (8, 2 * LOADS))
    square = jnp.concatenate([sums[:, LOADS:], sums[:, LOADS:]], axis=1)
    steps = sums / (square + 1e-06)
    step_ref[...] = steps[0, 0:LOADS]
    column = jnp.concatenate([steps] * 16, axis=0).T[0:LOADS, 0:1]
    comps = [slice(c * LOADS, (c + 1) * LOADS) for c in range(COMP)]
    leaving = []
    for chunk in range(CHUNKS):
        panels = pl.ds(chunk * BLK, BLK)
        normal, slide_a, slide_b = (
            field_ref[rows, panels] - column * residual_ref[rows, panels] for rows in comps
        )
        coeff = sorted_ref[3:4, panels]
        live = sorted_ref[4:5, panels]
        slip = jnp.sqrt(slide_a * slide_a + slide_b * slide_b + SLIP_EPS)
        stick = slip <= coeff * normal
        slid = jnp.maximum((normal + coeff * slip) / (1.0 + coeff * coeff), 0.0)
        pressed = jnp.where(stick, normal, slid)
        factor = jnp.where(stick, jnp.ones_like(slip), coeff * pressed / slip)
        out_ref[chunk, comps[0], :] = pressed * live
        out_ref[chunk, comps[1], :] = factor * slide_a * live
        out_ref[chunk, comps[2], :] = factor * slide_b * live
        copy = pltpu.make_async_copy(out_ref.at[chunk], out_hbm.at[:, panels], sems.at[chunk])
        copy.start()
        leaving.append(copy)
    for copy in leaving:
        copy.wait()


def final_step(got, field, residual, panel_rows, entries):
    return call(
        functools.partial(final_kernel, entries),
        "final",
        in_specs=[IN_VMEM] * 4,
        out_specs=[IN_HBM, IN_VMEM],
        out_shape=[FIELD, jax.ShapeDtypeStruct((LOADS,), F32)],
        scratch_shapes=[
            pltpu.VMEM((CHUNKS, ROWS, BLK), F32),
            pltpu.SemaphoreType.DMA((CHUNKS,)),
        ],
    )(in_vmem(got), in_vmem(field), in_vmem(residual), in_vmem(panel_rows))


def swap(blocks, axes):
    return lax.all_to_all(blocks, axes, 0, 0)


def beside(blocks):
    size = lax.axis_size(WIDE_NARROW)
    up = [(i, i + 1) for i in range(size - 1)]
    down = [(b, a) for a, b in up]
    return lax.ppermute(blocks, WIDE_NARROW, up), lax.ppermute(blocks, WIDE_NARROW, down)


def operator(place, low, sent, *early):
    sides = beside(low)
    got = swap(sent, NARROW)
    up = plane_sums(got)
    lower = lower_sums(place, got)
    upper, sides, early = lax.optimization_barrier((swap(up, WIDE), sides, early))
    return sides, swap(upper_sums(place, upper, lower), NARROW), early


def body(
    traction,
    near_kernel,
    neighbours,
    far_basis,
    surface_gap,
    friction,
    contact_flags,
    cluster_order,
    approach,
):
    field = traction.reshape(ROWS, PAN)
    place = jnp.stack([lax.axis_index(NARROW), lax.axis_index(WIDE)]).astype(jnp.int32)
    panel_rows = jnp.concatenate(
        [
            surface_gap,
            friction[None],
            contact_flags.astype(F32)[None],
            jnp.zeros((3, PAN), F32),
        ]
    )
    panel_rows = sort_panels(cluster_order[None], panel_rows)

    low, sent = first_coefs(field, far_basis)
    (left, right), coefs, (panel_rows,) = operator(place, low, sent, panel_rows)
    near = near_field(
        neighbours, left, low, right, near_kernel, approach, in_hbm(panel_rows)
    )
    residual, low, sent = residual_step(coefs, near, far_basis)
    (left, right), coefs, _ = operator(place, low, sent)
    near = near_field(neighbours, left, low, right, near_kernel)
    sums = local_products(coefs, near, residual, far_basis)

    devices = lax.axis_size(WIDE_NARROW)
    sums = swap(jnp.broadcast_to(sums[None], (devices, 1, 2 * LOADS)), WIDE_NARROW)
    entries = COMP * PAN * devices
    updated, steps = final_step(sums, field, residual, panel_rows, entries)
    shape = (COMP, LOADS, PAN)
    return updated.reshape(shape), residual.reshape(shape), steps


def solution(mesh):
    finer = Mesh(mesh.devices.reshape(8, 2, 4, 4), ("wide_0", "wide_1", "narrow_0", "narrow_1"))
    placed = (
        P(None, None, WIDE_NARROW),
        P(WIDE_NARROW, None, None, None),
        P(WIDE_NARROW, None),
        P(None, WIDE_NARROW, None),
        P(None, WIDE_NARROW),
        P(WIDE_NARROW),
        P(WIDE_NARROW),
        P(WIDE_NARROW),
        P(),
    )
    return jax.shard_map(
        body,
        mesh=finer,
        in_specs=placed,
        out_specs=(P(None, None, WIDE_NARROW), P(None, None, WIDE_NARROW), P()),
        check_vma=False,
    )
```
